256 devices in a mesh: ctx: 4 (over y), sp: 32 (over z, x_lo, core), dp: 2 (over x_hi).
Axes of the slice: x: 4 (x_hi: 2, x_lo: 2; x = x_hi * 2 + x_lo), y: 4, z: 8, core: 2. Of those that a mesh axis runs over, the one named last changes fastest.
Arguments:
- resid: bfloat16 [32768, 2048], P(('dp', 'ctx', 'sp')), parts along dimension 0, may hold values from -6 to 6
- conv_weight: bfloat16 [4, 2048], replicated, may hold values from -3 to 3
- queries: bfloat16 [32768, 2048], P(('dp', 'ctx', 'sp')), parts along dimension 0, may hold values from -100 to 100
- keys: bfloat16 [32768, 256], P(('dp', 'ctx', 'sp')), parts along dimension 0, may hold values from -5 to 5
- values: bfloat16 [32768, 256], P(('dp', 'ctx', 'sp')), parts along dimension 0, may hold values from -6 to 6
- gates: bfloat16 [32768, 2048], P(('dp', 'ctx', 'sp')), parts along dimension 0, may hold values from -6 to 6
- out_weight: bfloat16 [2048, 2048], P('sp'), may hold values from -0.125 to 0.125
- norm_gain: float32 [2048], replicated, may hold values from 0.5 to 1.5
- lens_weight: bfloat16 [2048, 81920], P(None, ('ctx', 'sp')), may hold values from -0.41992188 to 0.41992188
Outputs:
- mixed: bfloat16 [32768, 2048], P(('dp', 'ctx', 'sp')), parts along dimension 0
- lens_logits: float32 [2048, 81920], P('dp', ('ctx', 'sp')), parts along dimension 0
The draws below stay inside these ranges and needn't reach their ends.
There are 2 independent parts, one for each index of `dp`. The reference program is written for one: setup_inputs(seed, part) draws one part's arguments, and reference() takes and returns one part's arrays. A program takes and returns all parts, laid end to end along the dimension named above; an argument that names none is the same for every part. Nothing has to cross between parts.
All inputs are finite; a program needn't handle non-finite values.
Results may differ from the reference program's by a relative error of at most 0.013.
Values may be sent and summed in bfloat16 or wider, within the bound.
No kernel may reach another device: no remote copies, remote signals or barrier semaphores. Data moves between devices by JAX's collectives and lax.ppermute only.
A program may use at most 128 MiB of HBM per device.

```python
import math
import jax
import jax.numpy as jnp
from jax import lax

D = 2048
HEADS = 8
HD = 256
KERNEL = 4
TOK_DEV = 128
LENS_DEV = 8
SEQ = 16384
VOCAB = 81920
N_CTX = 4
N_SP = 32


def shared_rows(key):
    return jnp.clip(jax.random.normal(key, (SEQ, HD), jnp.float32), -5.0, 5.0)


def draw_keys(key, part):
    common = shared_rows(key)
    return common.astype(jnp.bfloat16)


def draw_queries(key, part):
    key = jax.random.fold_in(key, 7)
    spread = 3.0 * jnp.clip(jax.random.normal(key, (SEQ, HEADS, HD), jnp.float32), -4.0, 4.0)
    return spread.reshape(SEQ, HEADS * HD).astype(jnp.bfloat16)


def levels(own_key, extent, split, smallest, largest):
    level, own = 1.0, jax.random.fold_in(own_key, 6)
    for axis_at, shards_of in split:
        draws = jnp.exp(jax.random.uniform(jax.random.fold_in(own, axis_at), (shards_of,), jnp.float32, smallest / len(split), largest / len(split)))
        level = level * jnp.repeat(draws, extent[axis_at] // shards_of).reshape([-1 if axis == axis_at else 1 for axis in range(len(extent))])
    return level


def gaussian(rng, shape, deviation, reach, pieces=(), held_as=jnp.bfloat16):
    drawn = jax.random.normal(rng, shape, jnp.float32) * deviation
    if len(pieces) > 0:
        drawn = levels(rng, shape, pieces, -0.22, 0.18) * drawn
    return jnp.clip(drawn, min=-reach, max=reach).astype(held_as)


def setup_inputs(seed: int = 0, part: int = 0) -> dict:
    key_of = jax.random.split(jax.random.key(seed), 10)
    part_keys = jax.random.split(jax.random.fold_in(key_of[9], part), 10)
    return {
        "resid": gaussian(part_keys[0], (SEQ, D), 1.0, 6.0, ((0, 128),)),
        "conv_weight": gaussian(key_of[1], (KERNEL, D), 0.5, 3.0),
        "queries": draw_queries(jax.random.fold_in(jax.random.fold_in(key_of[9], part), 71), part),
        "keys": draw_keys(jax.random.fold_in(jax.random.fold_in(key_of[9], part), 71), part),
        "values": gaussian(part_keys[4], (SEQ, HD), 1.0, 6.0, ((0, 128),)),
        "gates": gaussian(part_keys[5], (SEQ, HEADS * HD), 1.0, 6.0, ((0, 128),)),
        "out_weight": gaussian(key_of[6], (HEADS * HD, D), (HEADS * HD) ** -0.5, 0.125, ((0, 32),)),
        "norm_gain": jnp.clip(1.0 + 0.1 * jax.random.normal(key_of[7], (D,), jnp.float32), 0.5, 1.5),
        "lens_weight": gaussian(key_of[8], (D, VOCAB), 0.07, 0.41992188, ((1, 128),)),
    }


NEG_FILL = -1e+30

def reference(resid, conv_weight, queries, keys, values, gates, out_weight, norm_gain, lens_weight):
    dev_count = N_CTX * N_SP
    half_len = TOK_DEV // 2
    places = jnp.arange(SEQ, dtype=jnp.int32)
    stretch_idx = places // half_len
    is_early = stretch_idx < dev_count
    holder = jnp.where(is_early, stretch_idx, 2 * dev_count - 1 - stretch_idx)
    offset_in = jnp.where(is_early, places % half_len, half_len + places % half_len)
    source = (holder * TOK_DEV + offset_in).astype(jnp.int32)
    stored_dev = places // TOK_DEV
    stored_in = places % TOK_DEV
    position = jnp.where(stored_in < half_len, stored_dev * half_len + stored_in, (2 * dev_count - 1 - stored_dev) * half_len + stored_in - half_len).astype(jnp.int32)
    resid_pos = resid[source].astype(jnp.float32)
    padded = jnp.pad(resid_pos, ((KERNEL - 1, 0), (0, 0)))
    conv_sum = jnp.zeros((SEQ, D), jnp.float32)
    for tap_index in range(KERNEL):
        conv_sum = conv_sum + conv_weight[tap_index].astype(jnp.float32) * padded[KERNEL - 1 - tap_index:KERNEL - 1 - tap_index + SEQ]
    hidden = (resid_pos + jax.nn.silu(conv_sum)).astype(jnp.bfloat16)
    query_pos = queries[source].reshape(SEQ, HEADS, HD).astype(jnp.float32)
    key_pos = keys[source].astype(jnp.float32)
    value_pos = values[source].astype(jnp.float32)
    block_rows = math.gcd(SEQ, 256)
    key_index = jnp.arange(SEQ, dtype=jnp.int32)

    def attend_block(block_id):
        first_row = (block_id * block_rows).astype(jnp.int32)
        query_blk = lax.dynamic_slice_in_dim(query_pos, first_row, block_rows, 0)
        scores = jnp.einsum('qhd,kd->qhk', query_blk, key_pos) / math.sqrt(HD)
        row_index = first_row + jnp.arange(block_rows, dtype=jnp.int32)
        visible = key_index[None, None, :] <= row_index[:, None, None]
        scores = jnp.where(visible, scores, NEG_FILL)
        row_max = lax.optimization_barrier(jnp.max(scores, axis=-1, keepdims=True))
        probs = jnp.exp(scores - row_max)
        denom = lax.optimization_barrier(jnp.sum(probs, axis=-1))
        rounded = lax.optimization_barrier(probs.astype(jnp.bfloat16))
        numer = jnp.einsum('qhk,kd->qhd', rounded.astype(jnp.float32), value_pos)
        return (numer / denom[..., None]).reshape(block_rows, HEADS * HD)
    att = lax.map(attend_block, jnp.arange(SEQ // block_rows, dtype=jnp.int32)).reshape(SEQ, HEADS * HD)
    gated_rows = (jax.nn.sigmoid(gates[source].astype(jnp.float32)) * att).astype(jnp.bfloat16)
    mixed_pos = (hidden.astype(jnp.float32) + jnp.dot(gated_rows, out_weight, preferred_element_type=jnp.float32)).astype(jnp.bfloat16)
    mixed = mixed_pos[position]
    stride = TOK_DEV // LENS_DEV
    selected = mixed.reshape(SEQ // stride, stride, D)[:, stride - 1].astype(jnp.float32)
    normed = (selected * lax.rsqrt(lax.optimization_barrier(jnp.mean(selected * selected, axis=-1, keepdims=True)) + 1e-06) * norm_gain).astype(jnp.bfloat16)
    lens_logits = jnp.dot(normed, lens_weight, preferred_element_type=jnp.float32)
    return (mixed, lens_logits)
```

```python
import functools
import math

import jax
import jax.numpy as jnp
from jax import lax
from jax.experimental import pallas as pl
from jax.experimental.pallas import tpu as pltpu
from jax.sharding import Mesh
from jax.sharding import PartitionSpec as P

NY, NZ, NX, NC = 4, 8, 2, 2
HEADS, HD = 8, 256
HALF = 64
TEAM = NX * NC
SUPER = TEAM * HALF
CHUNKS = 2 * NY * NZ
NEG = -1e30
LOG2E = math.log2(math.e)
BK = 512
BF = jnp.bfloat16
F32 = jnp.float32


def shift(x, axis, by, count):
    return lax.ppermute(x, axis, [(i, (i + by) % count) for i in range(count)])


def moved(entries, axis, delta):
    return [(tuple(o + (delta if a == axis else 0) for a, o in enumerate(off)), r0, n) for off, r0, n in entries]


AXES = {"y": (0, NY), "z": (1, NZ), "xl": (2, NX)}


def joined(pieces):
    arrays = [p[0] for p in pieces]
    entries = [e for p in pieces for e in p[1]]
    return (arrays[0] if len(arrays) == 1 else jnp.concatenate(arrays, 0)), entries


def split(x, entries):
    rows = x.shape[0]
    if len(entries) % 2 == 0:
        k = len(entries) // 2
        low, high = entries[:k], entries[k:]
    else:
        assert len(entries) == 1
        off, r0, n = entries[0]
        low, high = [(off, r0, n // 2)], [(off, r0 + n // 2, n // 2)]
    return (x[: rows // 2], low), (x[rows // 2 :], high)


def hop(piece, name, by):
    axis, count = AXES[name]
    return shift(piece[0], name, by, count), moved(piece[1], axis, -by)


def pair(piece, name="xl"):
    return [piece, hop(piece, name, 1)]


def direct(piece, name):
    count = AXES[name][1]
    return [piece] + [hop(piece, name, s) for s in range(1, count)]


def two_step(piece, name="z"):
    a, b = hop(piece, name, 1), hop(piece, name, -1)
    c, d = hop(piece, name, 2), hop(piece, name, -2)
    e, f = hop(c, name, 1), hop(d, name, -1)
    g = hop(split(*c)[0], name, 2)
    h = hop(split(*d)[1], name, -2)
    return [piece, a, b, c, d, e, f, g, h]


def ring(piece, name):
    count = AXES[name][1]
    out, fwd, bwd = [piece], piece, piece
    for _ in range(count // 2 - 1):
        fwd, bwd = hop(fwd, name, 1), hop(bwd, name, -1)
        out += [fwd, bwd]
    return out + [hop(split(*fwd)[0], name, 1), hop(split(*bwd)[1], name, -1)]


def wrapped(entry, y, z, xl):
    off = entry[0]
    return (y + off[0]) % NY, (z + off[1]) % NZ, (xl + off[2]) % NX


def attention_kernel(layout, place, *refs):
    n_in = len(layout)
    q_refs, kv_refs = refs[:TEAM], refs[TEAM : TEAM + n_in]
    keep_ref, send_ref, lse_ref = refs[TEAM + n_in : TEAM + n_in + 3]
    kvs, qs, acc, m_s, l_s, sems = refs[TEAM + n_in + 3 :]
    half = pl.program_id(0)
    y, z, xl, c = place[0], place[1], place[2], place[3]
    j = y * NZ + z
    k = xl * NC + c
    late = half == 1
    block = jnp.where(late, CHUNKS - 1 - j, j)

    @pl.when(half == 0)
    def _():
        copies = []
        for ref, (is_late, entries) in zip(kv_refs, layout):
            at = 0
            for off, r0, n in entries:
                jj = ((y + off[0] + NY) & (NY - 1)) * NZ + ((z + off[1] + NZ) & (NZ - 1))
                slot = (CHUNKS - 1 - jj) if is_late else jj
                dst = kvs.at[pl.ds(pl.multiple_of(slot * HALF + r0, 16), n)]
                copies.append(pltpu.make_async_copy(ref.at[pl.ds(at, n)], dst, sems.at[len(copies)]))
                at += n
        for cp in copies:
            cp.start()
        for cp in copies:
            cp.wait()

    for h in range(HEADS):
        for r in range(TEAM):
            rows = q_refs[r][pl.ds(pl.multiple_of(half * HALF, HALF), HALF), h * HD : (h + 1) * HD]
            qs[h, r * HALF : (r + 1) * HALF, :] = rows * BF(1.0 / math.sqrt(HD))
    acc[...] = jnp.zeros_like(acc)
    m_s[...] = jnp.full_like(m_s, NEG)
    l_s[...] = jnp.zeros_like(l_s)
    per = BK // HALF

    def step(b, masked):
        start = pl.multiple_of(b * BK, BK)
        kb = kvs[pl.ds(start, BK), :HD]
        vb = kvs[pl.ds(start, BK), HD:]
        if masked:
            idx = start + lax.broadcasted_iota(jnp.int32, (SUPER, BK), 1)
            sub_k = jnp.where(idx >= CHUNKS // 2 * HALF, TEAM - 1 - k, k)
            k_pos = (idx >> 6) * SUPER + sub_k * HALF + (idx & (HALF - 1))
            row = lax.broadcasted_iota(jnp.int32, (SUPER, BK), 0)
            member = (row >> 6) ^ k
            sub_q = jnp.where(late, TEAM - 1 - member, member)
            q_pos = block * SUPER + sub_q * HALF + (row & (HALF - 1))
            visible = k_pos <= q_pos
        for h in range(HEADS):
            s = lax.dot_general(qs[h], kb, (((1,), (1,)), ((), ())), preferred_element_type=F32)
            if masked:
                s = jnp.where(visible, s, NEG)
            m_old = m_s[h]
            mx = s[:, :128]
            for t in range(1, BK // 128):
                mx = jnp.maximum(mx, s[:, t * 128 : (t + 1) * 128])
            m_new = jnp.maximum(m_old, jnp.max(mx, axis=1, keepdims=True))
            alpha = jnp.exp2((m_old - m_new) * LOG2E)
            m_s[h] = m_new
            parts, total = [], l_s[h] * alpha
            for t in range(BK // 128):
                p = jnp.exp2((s[:, t * 128 : (t + 1) * 128] - m_new) * LOG2E)
                total = total + p
                parts.append(p.astype(BF))
            l_s[h] = total
            o = jnp.dot(jnp.concatenate(parts, 1), vb, preferred_element_type=F32)
            acc[h] = acc[h] * jnp.concatenate([alpha, alpha], 1) + o

    full = block // per

    def body(b, carry):
        step(b, False)
        return carry

    lax.fori_loop(0, full, body, 0)
    step(full, True)
    lane = lax.broadcasted_iota(jnp.int32, (SUPER, 128), 1)
    lse = jnp.zeros((SUPER, 128), F32)
    for h in range(HEADS):
        total = jnp.sum(l_s[h], axis=1, keepdims=True)
        o = acc[h] / total
        lse = jnp.where(lane == h, m_s[h] + jnp.log(total), lse)
        a, b = o[:, :128], o[:, 128:]
        cols = slice(h * 128, (h + 1) * 128)
        keep_ref[:, :, cols] = jnp.where(c == 0, a, b).astype(BF).reshape(TEAM, HALF, 128)
        send_ref[:, :, cols] = jnp.where(c == 0, b, a).astype(BF).reshape(TEAM, HALF, 128)
    lse_ref[0] = lse.T[:HEADS]


def attention(place, q_team, kv):
    tok, width = q_team[0].shape
    layout = [(is_late, entries) for _, is_late, entries in kv]
    n_copies = sum(len(e) for _, e in layout)
    return pl.pallas_call(
        functools.partial(attention_kernel, layout),
        grid_spec=pltpu.PrefetchScalarGridSpec(
            num_scalar_prefetch=1,
            grid=(2,),
            in_specs=[pl.BlockSpec((tok, width), lambda i, p: (0, 0))] * TEAM
            + [pl.BlockSpec(memory_space=pl.ANY)] * len(kv),
            out_specs=[pl.BlockSpec((TEAM, HALF, HEADS * 128), lambda i, p: (0, i, 0))] * 2
            + [pl.BlockSpec((1, HEADS, SUPER), lambda i, p: (i, 0, 0))],
            scratch_shapes=[
                pltpu.VMEM((CHUNKS * HALF, 2 * HD), BF),
                pltpu.VMEM((HEADS, SUPER, HD), BF),
                pltpu.VMEM((HEADS, SUPER, HD), F32),
                pltpu.VMEM((HEADS, SUPER, 128), F32),
                pltpu.VMEM((HEADS, SUPER, 128), F32),
                pltpu.SemaphoreType.DMA((n_copies,)),
            ],
        ),
        out_shape=[
            jax.ShapeDtypeStruct((TEAM, tok, HEADS * 128), BF),
            jax.ShapeDtypeStruct((TEAM, tok, HEADS * 128), BF),
            jax.ShapeDtypeStruct((2, HEADS, SUPER), F32),
        ],
        compiler_params=pltpu.CompilerParams(vmem_limit_bytes=40 * 2**20),
        cost_estimate=pl.CostEstimate(flops=10**10, bytes_accessed=8 * 2**20, transcendentals=10**7),
    )(place, *q_team, *[a for a, _, _ in kv])


def by_row(lse):
    return jnp.concatenate([lse, jnp.zeros((128 - lse.shape[0], lse.shape[1]), F32)], 0).T


def join_kernel(keep_ref, recv_ref, lse_ref, lse_recv_ref, mine_ref, other_ref, lse_out_ref):
    lane = lax.broadcasted_iota(jnp.int32, (HALF, 128), 1)
    for half in range(2):
        own, theirs = by_row(lse_ref[half]), by_row(lse_recv_ref[half])
        rows = slice(half * HALF, (half + 1) * HALF)
        joint = []
        for r in range(TEAM):
            a = own[r * HALF : (r + 1) * HALF]
            b = theirs[(r ^ 1) * HALF : ((r ^ 1) + 1) * HALF]
            m = jnp.maximum(a, b)
            wa, wb = jnp.exp(a - m), jnp.exp(b - m)
            total = wa + wb
            wa, wb = wa / total, wb / total
            joint.append(m + jnp.log(total))
            for h in range(HEADS):
                cols = slice(h * 128, (h + 1) * 128)
                o = keep_ref[r, rows, cols].astype(F32) * wa[:, h : h + 1]
                o = o + recv_ref[r ^ 1, rows, cols].astype(F32) * wb[:, h : h + 1]
                if r < 2:
                    mine_ref[r, rows, cols] = o.astype(BF)
                else:
                    other_ref[r - 2, rows, cols] = o.astype(BF)
        lse_out_ref[half] = jnp.concatenate(joint, 0).T[:HEADS]


def join(keep, recv, lse, lse_recv):
    tok, width = keep.shape[1:]
    return pl.pallas_call(
        join_kernel,
        out_shape=[
            jax.ShapeDtypeStruct((2, tok, width), BF),
            jax.ShapeDtypeStruct((2, tok, width), BF),
            jax.ShapeDtypeStruct(lse.shape, F32),
        ],
        compiler_params=pltpu.CompilerParams(vmem_limit_bytes=32 * 2**20),
    )(keep, recv, lse, lse_recv)


def project_kernel(layout, place, mine_ref, recv_ref, lse_ref, lse_recv_ref, g0_ref, g1_ref, *refs):
    w_refs = refs[: len(layout)]
    keep_ref, send_ref, ws, gated, sems = refs[len(layout) :]
    y, z = place[0], place[1]
    copies = []
    for ref, (base, entries) in zip(w_refs, layout):
        at = 0
        for off, r0, n in entries:
            head = (z + off[1] + NZ) & (NZ - 1)
            row = head * 128 + base + r0
            if base:
                row = row + ((y + off[0] + NY) & (NY - 1)) * 16
            dst = ws.at[pl.ds(pl.multiple_of(row, 16), n)]
            copies.append(pltpu.make_async_copy(ref.at[pl.ds(at, n)], dst, sems.at[len(copies)]))
            at += n
    for cp in copies:
        cp.start()
    tok = keep_ref.shape[0]
    for half in range(2):
        own, theirs = by_row(lse_ref[half]), by_row(lse_recv_ref[half])
        rows = slice(half * HALF, (half + 1) * HALF)
        for r in range(2):
            a = own[r * HALF : (r + 1) * HALF]
            b = theirs[(r + 2) * HALF : (r + 3) * HALF]
            m = jnp.maximum(a, b)
            wa, wb = jnp.exp(a - m), jnp.exp(b - m)
            total = wa + wb
            wa, wb = wa / total, wb / total
            g_ref = (g0_ref, g1_ref)[r]
            for h in range(HEADS):
                cols = slice(h * 128, (h + 1) * 128)
                o = mine_ref[r, rows, cols].astype(F32) * wa[:, h : h + 1]
                o = o + recv_ref[r, rows, cols].astype(F32) * wb[:, h : h + 1]
                o = jax.nn.sigmoid(g_ref[rows, cols].astype(F32)) * o
                gated[r * tok + half * HALF : r * tok + (half + 1) * HALF, cols] = o.astype(BF)
    for cp in copies:
        cp.wait()
    step = 512

    @pl.loop(0, keep_ref.shape[1] // step)
    def _(n):
        cols = pl.ds(pl.multiple_of(n * step, step), step)
        out = jnp.dot(gated[...], ws[:, cols], preferred_element_type=F32)
        keep_ref[:, cols] = out[:tok]
        send_ref[:, cols] = out[tok:].astype(BF)


def project(place, mine, recv, lse, lse_recv, g0, g1, weights):
    tok = mine.shape[1]
    width = weights[0][0].shape[1]
    layout = [(base, entries) for _, base, entries in weights]
    n_copies = sum(len(e) for _, e in layout)
    vm = pl.BlockSpec(memory_space=pltpu.VMEM)
    return pl.pallas_call(
        functools.partial(project_kernel, layout),
        in_specs=[pl.BlockSpec(memory_space=pltpu.SMEM)] + [vm] * 6 + [pl.BlockSpec(memory_space=pl.ANY)] * len(weights),
        out_specs=[vm, vm],
        out_shape=[jax.ShapeDtypeStruct((tok, width), F32), jax.ShapeDtypeStruct((tok, width), BF)],
        scratch_shapes=[
            pltpu.VMEM((HEADS * 128, width), BF),
            pltpu.VMEM((2 * tok, HEADS * 128), BF),
            pltpu.SemaphoreType.DMA((n_copies,)),
        ],
        compiler_params=pltpu.CompilerParams(vmem_limit_bytes=32 * 2**20),
    )(place, mine, recv, lse, lse_recv, g0, g1, *[a for a, _, _ in weights])


def lens_kernel(pos_ref, x0_ref, x1_ref, x2_ref, x3_ref, w_ref, out_ref):
    depth = x0_ref.shape[1]
    tile = 128
    for src, ref in enumerate((x0_ref, x1_ref, x2_ref, x3_ref)):
        part = src % 2

        @pl.loop(0, ref.shape[0] // tile)
        def _(m, src=src, ref=ref, part=part):
            x = ref[pl.ds(pl.multiple_of(m * tile, tile), tile), :]
            got = jnp.dot(x, w_ref[part * depth : (part + 1) * depth, :], preferred_element_type=F32)
            for g in range(tile // 8):
                at = pl.ds(pl.multiple_of(pos_ref[src, m * (tile // 8) + g] * 8, 8), 8)
                if part == 0:
                    out_ref[at, :] = got[g * 8 : (g + 1) * 8]
                else:
                    out_ref[at, :] = out_ref[at, :] + got[g * 8 : (g + 1) * 8]


def lens_matmul(pos, xs, weight):
    vm = pl.BlockSpec(memory_space=pltpu.VMEM)
    rows = 2 * xs[0].shape[0]
    return pl.pallas_call(
        lens_kernel,
        in_specs=[pl.BlockSpec(memory_space=pltpu.SMEM)] + [vm] * 5,
        out_specs=vm,
        out_shape=jax.ShapeDtypeStruct((rows, weight.shape[1]), F32),
        compiler_params=pltpu.CompilerParams(vmem_limit_bytes=40 * 2**20),
    )(pos, *xs, weight)


def short_conv(prefix, rows, taps):
    lag = taps.shape[0] - 1
    extended = jnp.concatenate([prefix, rows], 0).astype(F32)
    total = jnp.zeros(rows.shape, F32)
    for t in range(lag + 1):
        total = total + taps[t].astype(F32) * extended[lag - t : lag - t + rows.shape[0]]
    return total


def hidden_rows(resid, taps, me, last):
    lag = taps.shape[0] - 1
    count = NY * NZ * NX * NC
    names = ("y", "z", "xl", "c")
    low = lax.ppermute(resid[HALF - lag : HALF], names, [(i, i + 1) for i in range(count - 1)])
    high = lax.ppermute(resid[2 * HALF - lag :], names, [(i + 1, i) for i in range(count - 1)])
    high = jnp.where(me == last, resid[HALF - lag : HALF], high)
    conv = jnp.concatenate([short_conv(low, resid[:HALF], taps), short_conv(high, resid[HALF:], taps)], 0)
    return (resid.astype(F32) + jax.nn.silu(conv)).astype(BF)


def body(resid, conv_weight, queries, keys, values, gates, out_weight, norm_gain, lens_weight):
    y, z, xl, c = (lax.axis_index(a) for a in ("y", "z", "xl", "c"))
    me = ((y * NZ + z) * NX + xl) * NC + c
    k = xl * NC + c
    place = jnp.stack([y, z, xl, c]).astype(jnp.int32)
    swap = lambda x: shift(x, "c", 1, NC)
    cross = lambda x: shift(x, "xl", 1, NX)
    here = (0, 0, 0)
    tok = resid.shape[0]

    kv_own = jnp.concatenate([keys, values], 1)
    early = two_step((kv_own[:HALF], [(here, 0, HALF)]), "z")
    late = joined(direct((kv_own[HALF:], [(here, 0, HALF)]), "y"))
    late = ring(late, "z")
    early = direct(joined(early), "y")
    kv = [(a, False, e) for a, e in early] + [(a, True, e) for a, e in late]

    q1, q2 = swap(queries), cross(queries)
    q3 = swap(q2)

    pairs = gates.reshape(tok, HEADS, 2, 128)
    g_keep = jnp.where(c == 0, pairs[:, :, 0], pairs[:, :, 1]).reshape(tok, HEADS * 128)
    g_send = jnp.where(c == 0, pairs[:, :, 1], pairs[:, :, 0]).reshape(tok, HEADS * 128)
    g_other = swap(g_send)

    team = ("xl", "c")
    p1 = lax.ppermute(out_weight, team, [(1, 0), (2, 3)])
    p2 = lax.ppermute(out_weight, team, [(0, 2), (3, 1)])
    p3 = lax.ppermute(out_weight, team, [(1, 2), (2, 1)])
    pick = lambda a, b, d, e: jnp.where(k == 0, a, jnp.where(k == 1, b, jnp.where(k == 2, d, e)))
    w_low = pick(out_weight, p3, p2, p1)
    w_high = pick(p1, p2, p3, out_weight)
    n_low = w_low.shape[0]
    w_a = ring((w_low, [(here, 0, n_low)]), "z")
    quarter = lax.dynamic_slice_in_dim(w_high, y * (n_low // NY), n_low // NY, 0)
    w_b = joined(two_step((quarter, [(here, 0, n_low // NY)]), "z")) if False else joined(direct((quarter, [(here, 0, n_low // NY)]), "z"))
    w_b = direct(w_b, "y")
    weights = [(a, 0, e) for a, e in w_a] + [(a, n_low, e) for a, e in w_b]

    hidden = hidden_rows(resid, conv_weight, me, NY * NZ * NX * NC - 1)

    keep, send, lse = attention(place, [queries, q1, q2, q3], kv)
    mine, other, lse = join(keep, swap(send), lse, swap(lse))
    p_keep, p_send = project(place, mine, cross(other), lse, cross(lse), g_keep, g_other, weights)
    mixed = (hidden.astype(F32) + p_keep + swap(p_send).astype(F32)).astype(BF)

    lens_rows = tok // 16
    rows = mixed.reshape(lens_rows, 16, -1)[:, 15].astype(F32)
    normed = (rows * lax.rsqrt(jnp.mean(rows * rows, axis=-1, keepdims=True) + 1e-6) * norm_gain).astype(BF)
    depth = normed.shape[1] // 2
    r1 = joined(direct((normed[:, :depth], [(here, 0, lens_rows)]), "y"))
    r1 = joined(pair(r1))
    r1 = joined(ring(r1, "z"))
    r2 = joined(direct((normed[:, depth:], [(here, 0, lens_rows)]), "z"))
    r2 = joined(pair(r2))
    r2 = joined(direct(r2, "y"))
    pos = []
    for who in (c, 1 - c):
        for _, entries in (r1, r2):
            offs = jnp.array([e[0] for e in entries], jnp.int32)
            yy, zz, xx = (y + offs[:, 0]) % NY, (z + offs[:, 1]) % NZ, (xl + offs[:, 2]) % NX
            pos.append(((yy * NZ + zz) * NX + xx) * NC + who)
    logits = lens_matmul(jnp.stack(pos), [r1[0], r2[0], swap(r1[0]), swap(r2[0])], lens_weight)
    return mixed, logits


def solution(mesh):
    fine = Mesh(mesh.devices.reshape(NY, NZ, NX, NC, -1), ("y", "z", "xl", "c", "dp"))
    rows = P(("dp", "y", "z", "xl", "c"), None)
    return jax.shard_map(
        body,
        mesh=fine,
        in_specs=(rows, P(), rows, rows, rows, rows, P(("z", "xl", "c"), None), P(), P(None, ("y", "z", "xl", "c"))),
        out_specs=(rows, P("dp", ("y", "z", "xl", "c"))),
        check_vma=False,
    )
```

```python
import functools
import math

import jax
import jax.numpy as jnp
from jax import lax
from jax.experimental import pallas as pl
from jax.experimental.pallas import tpu as pltpu
from jax.sharding import Mesh
from jax.sharding import PartitionSpec as P

NY, NZ, NX, NC = 4, 8, 2, 2
HEADS, HD = 8, 256
HALF = 64
TEAM = NX * NC
SPAN = NZ * NX * NC * HALF
NEG = -1e30
BK, HB = 1024, 4
BF = jnp.bfloat16
F32 = jnp.float32


def packed(block):
    hi = block.astype(BF)
    rest = block - hi.astype(F32)
    mid = rest.astype(BF)
    low = (rest - mid.astype(F32)).astype(BF)
    pad = jnp.zeros((16 - block.shape[0], block.shape[1]), F32)
    return [jnp.concatenate([p.astype(F32), pad], 0).astype(BF) for p in (hi, mid, low)]


def attention_kernel(layout, place, *refs):
    n_kv = len(layout)
    q_refs, kv_refs, refs = refs[: NY + 1], refs[NY + 1 : NY + 1 + n_kv], refs[NY + 1 + n_kv :]
    outs, few_outs, refs = refs[: NY + 1], refs[NY + 1 : 2 * NY + 1], refs[2 * NY + 1 :]
    kvs, qs, acc, m_s, l_s, stage, ahead, sems = refs
    y, z, xl, c = place[0], place[1], place[2], place[3]
    copies = []

    def copy(src, dst):
        copies.append(pltpu.make_async_copy(src, dst, sems.at[len(copies)]))

    for ref, dy, halves in zip(q_refs, (0, 1, 3, 2, 2), ((0, 1), (0, 1), (0, 1), (0,), (1,))):
        for i, half in enumerate(halves):
            copy(ref.at[pl.ds(i * HALF, HALF)], qs.at[half * NY + ((y + dy) & (NY - 1))])
    for ref, entries in zip(kv_refs, layout):
        for at, (dz, dx, dc, r0, rows) in entries:
            s = (((z + dz) & (NZ - 1)) * NX + (xl ^ dx)) * NC + (c ^ dc)
            for half in range(2):
                low, high = max(r0, half * HALF), min(r0 + rows, (half + 1) * HALF)
                if low < high:
                    slot = (2 * NZ * NX * NC - 1 - s) if half else s
                    dst = kvs.at[pl.ds(pl.multiple_of(slot * HALF + low - half * HALF, 16), high - low)]
                    copy(ref.at[pl.ds(at + low - r0, high - low)], dst)
    for cp in copies:
        cp.start()
    m_s[...] = jnp.full_like(m_s, NEG)
    l_s[...] = jnp.zeros_like(l_s)
    acc[...] = jnp.zeros_like(acc)
    for cp in copies:
        cp.wait()

    qs[...] = qs[...] * BF(1.0 / math.sqrt(HD))
    tile = HB * HALF
    per = SPAN // BK
    me = (z * NX + xl) * NC + c
    early = me // (BK // HALF) + 1
    late = (NZ * NX * NC - 1 - me) // (BK // HALF) + 1
    n_whole = (2 * NY - 1) * per
    n_items = n_whole + early + late

    def place_of(i):
        e = i - NY * per
        f = e - (NY - 1 - y) * per
        p = i - n_whole
        g = jnp.where(e < 0, NY + i // per, jnp.where(f < 0, y + 1 + e // per, NY + f // per))
        kb = jnp.where(e < 0, i % per, jnp.where(f < 0, e % per, per + f % per))
        g = jnp.where(p < 0, g, jnp.where(p < early, y, NY + y))
        kb = jnp.where(p < 0, kb, jnp.where(p < early, p, per + p - early))
        return g, pl.multiple_of(kb * BK, BK)

    def scores(g, start, i):
        q = jnp.concatenate([qs[g, :, h * HD : (h + 1) * HD] for h in range(i * HB, (i + 1) * HB)], 0)
        return lax.dot_general(q, kvs[pl.ds(start, BK), :HD], (((1,), (1,)), ((), ())), preferred_element_type=F32)

    def fold(g, start, i, s, masked):
        rows = slice(i * tile, (i + 1) * tile)
        if masked:
            idx = start + lax.broadcasted_iota(jnp.int32, (HALF, BK), 1)
            k_pos = idx + jnp.where(idx < SPAN, y * SPAN, (2 * NY - 2 - y) * SPAN)
            row = lax.broadcasted_iota(jnp.int32, (HALF, BK), 0)
            st = (g & (NY - 1)) * (NZ * NX * NC) + me
            q_pos = jnp.where(g >= NY, 2 * NY * NZ * NX * NC - 1 - st, st) * HALF + row
            visible = k_pos <= q_pos
            s = jnp.concatenate([jnp.where(visible, s[h * HALF : (h + 1) * HALF], NEG) for h in range(HB)], 0)
        m_old = m_s[g, rows]
        mx = s[:, :128]
        for t in range(1, BK // 128):
            mx = jnp.maximum(mx, s[:, t * 128 : (t + 1) * 128])
        m_new = jnp.maximum(m_old, jnp.max(mx, axis=1, keepdims=True))
        alpha = jnp.exp(m_old - m_new)
        m_s[g, rows] = m_new
        parts, total = [], l_s[g, rows] * alpha
        for t in range(BK // 128):
            p = jnp.exp(s[:, t * 128 : (t + 1) * 128] - m_new)
            total = total + p
            parts.append(p.astype(BF))
        l_s[g, rows] = total
        v = kvs[pl.ds(start, BK), HD:]
        o = jnp.dot(jnp.concatenate(parts, 1), v, preferred_element_type=F32)
        acc[g, rows] = acc[g, rows] * jnp.concatenate([alpha, alpha], 1) + o

    def item(masked, i, carry):
        g, start = place_of(i)
        g_next, start_next = place_of(jnp.minimum(i + 1, n_items - 1))
        n = HEADS // HB
        s = ahead[...]
        for j in range(n):
            after = scores(g, start, j + 1) if j + 1 < n else scores(g_next, start_next, 0)
            fold(g, start, j, s, masked)
            s = after
        ahead[...] = s
        return carry

    ahead[...] = scores(*place_of(0), 0)
    lax.fori_loop(0, n_whole, functools.partial(item, False), 0)
    lax.fori_loop(n_whole, n_items, functools.partial(item, True), 0)

    lane = lax.broadcasted_iota(jnp.int32, (HALF, 128), 1)
    lane8 = lax.broadcasted_iota(jnp.int32, (8, 128), 1)
    pick = pl.ds(15, 4, stride=16)
    for dy in range(NY):
        lse = [jnp.zeros((HALF, 128), F32)] * 2
        few = jnp.zeros((8, 128), F32)
        for h in range(HEADS):
            rows = slice(h * HALF, (h + 1) * HALF)
            for half in range(2):
                g = half * NY + ((y + dy) & (NY - 1))
                total = jnp.maximum(jnp.sum(l_s[g, rows], axis=1, keepdims=True), 1e-30)
                value = m_s[g, rows] + jnp.log(total)
                lse[half] = jnp.where(lane == h, value, lse[half])
                o = acc[g, rows] * (1.0 / total)
                out, at = (outs[NY], 0) if dy == 2 and half else (outs[dy], half * HALF)
                out[at : at + HALF, h * HD : (h + 1) * HD] = o.astype(BF)
                stage[half * HALF : (half + 1) * HALF] = o[:, :128]
                stage[(2 + half) * HALF : (3 + half) * HALF] = o[:, 128:]
                stage[(4 + half) * HALF : (5 + half) * HALF] = value
            got = [stage[pl.ds(i * 2 * HALF + 15, 8, stride=16), :] for i in range(3)]
            few_outs[dy][:16, h * HD : (h + 1) * HD] = jnp.concatenate(
                [jnp.concatenate(got[:2], 1), jnp.zeros((8, HD), F32)], 0
            ).astype(BF)
            few = jnp.where(lane8 == h, got[2], few)
        block = jnp.concatenate(lse, 0).T[:HEADS]
        for out, blk, at in ((outs[NY], block, HALF) if dy == 2 else (outs[dy], block, 2 * HALF), (few_outs[dy], few, 16)):
            for p, v in enumerate(packed(blk)):
                out[at : at + 16, p * 128 : (p + 1) * 128] = v
            out[at : at + 16, 384:] = jnp.zeros((16, HEADS * HD - 384), BF)


def attention(place, qs, kv):
    tok, width = qs[0].shape
    layout = [e for _, e in kv]
    hbm = pl.BlockSpec(memory_space=pl.ANY)
    vm = pl.BlockSpec(memory_space=pltpu.VMEM)
    spans = [(r0, r0 + rows) for e in layout for _, (_, _, _, r0, rows) in e]
    n_copies = 2 * NY + sum(len([h for h in (0, 1) if max(a, h * HALF) < min(b, (h + 1) * HALF)]) for a, b in spans)
    return pl.pallas_call(
        functools.partial(attention_kernel, layout),
        in_specs=[pl.BlockSpec(memory_space=pltpu.SMEM)] + [hbm] * (len(qs) + len(kv)),
        out_specs=[vm] * (2 * NY + 1),
        out_shape=[jax.ShapeDtypeStruct((n, width), BF) for n in (tok + 16, tok + 16, HALF, tok + 16, HALF + 16)]
        + [jax.ShapeDtypeStruct((32, width), BF)] * NY,
        scratch_shapes=[
            pltpu.VMEM((2 * SPAN, 2 * HD), BF),
            pltpu.VMEM((2 * NY, HALF, width), BF),
            pltpu.VMEM((2 * NY, HEADS * HALF, HD), F32),
            pltpu.VMEM((2 * NY, HEADS * HALF, 128), F32),
            pltpu.VMEM((2 * NY, HEADS * HALF, 128), F32),
            pltpu.VMEM((6 * HALF, 128), F32),
            pltpu.VMEM((HB * HALF, BK), F32),
            pltpu.SemaphoreType.DMA((n_copies,)),
        ],
        compiler_params=pltpu.CompilerParams(vmem_limit_bytes=56 * 2**20),
        cost_estimate=pl.CostEstimate(flops=10**10, bytes_accessed=8 * 2**20, transcendentals=10**7),
    )(place, *qs, *[a for a, _ in kv])


def by_row(block, rows):
    if rows == 16:
        return jnp.concatenate([block, jnp.zeros((8, 128), F32)], 0)
    return jnp.concatenate([block, jnp.zeros((120, 128), F32)], 0).T


def join_kernel(rows, place, r0, r1, r2, r3, g_ref, keep_ref, send_ref):
    xl, c = place[2], place[3]
    refs = (r0, r1, r2, r3)
    blocks = []
    for r in refs:
        parts = [r[rows : rows + 16, p * 128 : (p + 1) * 128].astype(F32) for p in range(3)]
        blocks.append((parts[0] + parts[1] + parts[2])[:8])
    m = functools.reduce(jnp.maximum, blocks)
    exps = [jnp.exp(b - m) for b in blocks]
    total = exps[0] + exps[1] + exps[2] + exps[3]
    weights = [by_row(e / total, rows) for e in exps]
    low = lax.broadcasted_iota(jnp.int32, (rows, 128), 1) < 64
    for pair in range(HEADS // 2):
        quarters = []
        for h in (2 * pair, 2 * pair + 1):
            for t in range(2):
                cols = slice(h * HD + t * 128, h * HD + (t + 1) * 128)
                o = jnp.zeros((rows, 128), F32)
                for r, w in zip(refs, weights):
                    o = o + r[:rows, cols].astype(F32) * w[:, h : h + 1]
                quarters.append(jax.nn.sigmoid(g_ref[:, cols].astype(F32)) * o)
        cols = slice(pair * 128, (pair + 1) * 128)
        for t in range(2):
            a, b = quarters[t], quarters[2 + t]
            first = jnp.where(low, a, pltpu.roll(b, 64, 1))
            second = jnp.where(low, pltpu.roll(a, 64, 1), b)
            keep_ref[t ^ xl, :, cols] = jnp.where(c == 0, first, second).astype(BF)
            send_ref[t ^ xl, :, cols] = jnp.where(c == 0, second, first).astype(BF)


def join(place, parts, g):
    rows, width = g.shape
    vm = pl.BlockSpec(memory_space=pltpu.VMEM)
    half = jax.ShapeDtypeStruct((NX, rows, width // TEAM), BF)
    return pl.pallas_call(
        functools.partial(join_kernel, rows),
        in_specs=[pl.BlockSpec(memory_space=pltpu.SMEM)] + [vm] * 5,
        out_specs=[vm, vm],
        out_shape=[half, half],
        compiler_params=pltpu.CompilerParams(vmem_limit_bytes=24 * 2**20),
    )(place, *parts, g)


def project_kernel(rows, a_ref, b_ref, w0_hbm, w1_hbm, w2_hbm, keep_ref, send_ref, ws, sems):
    step = 512
    n = keep_ref.shape[1] // step
    loads = []
    for i in range(n):
        cols = slice(i * step, (i + 1) * step)
        at = 0
        for t, w in enumerate((w0_hbm, w1_hbm, w2_hbm)):
            n_rows = w.shape[0]
            loads.append(pltpu.make_async_copy(w.at[:, cols], ws.at[at : at + n_rows, cols], sems.at[i, t]))
            at += n_rows
    for load in loads:
        load.start()
    x = jnp.concatenate([jnp.concatenate([a_ref[t], b_ref[t]], 0) for t in range(NX)], 1)
    for i in range(n):
        for t in range(3):
            loads[3 * i + t].wait()
        cols = slice(i * step, (i + 1) * step)
        out = jnp.dot(x, ws[:, cols], preferred_element_type=F32)
        keep_ref[:, cols] = out[:rows]
        send_ref[:, cols] = out[rows:].astype(BF)


def project(a, b, w0, w1, w2):
    rows, width = a.shape[1], w0.shape[1]
    vm = pl.BlockSpec(memory_space=pltpu.VMEM)
    hbm = pl.BlockSpec(memory_space=pl.ANY)
    return pl.pallas_call(
        functools.partial(project_kernel, rows),
        in_specs=[vm, vm, hbm, hbm, hbm],
        out_specs=[vm, vm],
        out_shape=[jax.ShapeDtypeStruct((rows, width), F32), jax.ShapeDtypeStruct((rows, width), BF)],
        scratch_shapes=[pltpu.VMEM((NX * w0.shape[0], width), BF), pltpu.SemaphoreType.DMA((4, 3))],
        compiler_params=pltpu.CompilerParams(vmem_limit_bytes=24 * 2**20),
    )(a, b, w0, w1, w2)


def lens_kernel(who, x_ref, w_ref, *refs):
    out_ref = refs[-1]
    got = jnp.dot(x_ref[...], w_ref[...], preferred_element_type=F32)
    for i in range(out_ref.shape[0]):
        for j in range(NX):
            at = (i * NX + j) * NZ * 8
            out_ref[i, :, j, 0] = got[at : at + NZ * 8].reshape(NZ, 8, -1)


def lens(who, x, weight, before=None):
    ys = 2
    tile = ys * NX * NZ * 8
    rows, depth = x.shape
    vocab = weight.shape[1]
    extra = [] if before is None else [before]
    return pl.pallas_call(
        lens_kernel,
        grid_spec=pltpu.PrefetchScalarGridSpec(
            num_scalar_prefetch=1,
            grid=(rows // tile,),
            in_specs=[pl.BlockSpec((tile, depth), lambda i, w: (i, 0)), pl.BlockSpec((depth, vocab), lambda i, w: (0, 0))]
            + [pl.BlockSpec(memory_space=pl.ANY)] * len(extra),
            out_specs=pl.BlockSpec((ys, NZ, NX, 1, 8, vocab), lambda i, w: (i, 0, 0, w[0], 0, 0)),
        ),
        out_shape=jax.ShapeDtypeStruct((NY, NZ, NX, NC, 8, vocab), F32),
        input_output_aliases={} if before is None else {3: 0},
        compiler_params=pltpu.CompilerParams(vmem_limit_bytes=28 * 2**20),
        cost_estimate=pl.CostEstimate(flops=2 * rows * weight.size, bytes_accessed=6 * 2**20, transcendentals=0),
    )(who, x, weight, *extra)


def short_conv(prefix, rows, taps):
    lag = taps.shape[0] - 1
    extended = jnp.concatenate([prefix, rows], 0).astype(F32)
    total = jnp.zeros(rows.shape, F32)
    for t in range(lag + 1):
        total = total + taps[t].astype(F32) * extended[lag - t : lag - t + rows.shape[0]]
    return total


def hidden_rows(resid, rims, taps, me, last):
    lag = taps.shape[0] - 1
    count = NY * NZ * NX * NC
    names = ("y", "z", "xl", "c")
    low = lax.ppermute(rims[:lag], names, [(i, i + 1) for i in range(count - 1)])
    high = lax.ppermute(rims[lag:], names, [(i + 1, i) for i in range(count - 1)])
    high = jnp.where(me == last, resid[HALF - lag : HALF], high)
    conv = jnp.concatenate([short_conv(low, resid[:HALF], taps), short_conv(high, resid[HALF:], taps)], 0)
    return (resid.astype(F32) + jax.nn.silu(conv)).astype(BF)


def shift(x, axis, by):
    count = {"y": NY, "z": NZ, "xl": NX, "c": NC}[axis]
    return lax.ppermute(x, axis, [(i, (i + by) % count) for i in range(count)])


def body(resid, conv_weight, queries, keys, values, gates, out_weight, norm_gain, lens_weight):
    y, z, xl, c = (lax.axis_index(a) for a in ("y", "z", "xl", "c"))
    me = ((y * NZ + z) * NX + xl) * NC + c
    place = jnp.stack([y, z, xl, c]).astype(jnp.int32)
    tok, width = resid.shape
    few = lambda a: jnp.pad(a.reshape(8, 16, -1)[:, 15], ((0, 8), (0, 0)))

    w_own = lax.all_gather(out_weight, "z", axis=0, tiled=True)

    kv_own = jnp.concatenate([keys, values], 1)
    q_up, q_down = shift(queries, "y", -1), shift(queries, "y", 1)
    q_far = [shift(q_down[:HALF], "y", 1), shift(q_up[HALF:], "y", -1)]
    pair = jnp.concatenate([kv_own, shift(kv_own, "xl", 1)], 0)
    both = lambda dz: [(dz, 0, 0, 0, tok), (dz, 1, 0, 0, tok)]
    held = [(pair, both(0))]
    fwd = bwd = pair
    for s in range(1, NZ // 2):
        fwd, bwd = shift(fwd, "z", 1), shift(bwd, "z", -1)
        held += [(fwd, both(-s)), (bwd, both(s))]
    fwd, bwd = fwd[:tok], bwd[tok:]
    fwd, bwd, q_up, q_down, *q_far = lax.optimization_barrier((fwd, bwd, q_up, q_down, *q_far))
    held += [(shift(fwd, "z", 1), both(4)[:1]), (shift(bwd, "z", -1), both(4)[1:])]
    q_team = [queries, q_up, q_down] + q_far

    kv = []
    for group in (held[:5], held[5:]):
        entries, at = [], 0
        for piece, spans in group:
            kv.append((piece, [(i * tok, e) for i, e in enumerate(spans)]))
            for dz, dx, _, r0, n in spans:
                entries.append((at, (dz, dx, 1, r0, n)))
                at += n
        kv.append((shift(jnp.concatenate([p for p, _ in group], 0), "c", 1), entries))

    blocks = resid.reshape(8, 16, width)
    taps = conv_weight.astype(F32)
    conv_few = sum(taps[t] * blocks[:, 15 - t].astype(F32) for t in range(conv_weight.shape[0]))
    hidden_few = (blocks[:, 15].astype(F32) + jax.nn.silu(conv_few)).astype(BF)
    g_few = few(gates)
    half_w = w_own.shape[0] // 2
    w_other = [
        shift(w_own[:half_w], "xl", 1),
        lax.ppermute(w_own[half_w:], ("xl", "dp"), [(i, 3 - i) for i in range(4)]),
    ]
    place, hidden_few, g_few, _ = lax.optimization_barrier((place, hidden_few, g_few, w_own))
    got = attention(place, q_team, kv)
    main, lead = got[: NY + 1], got[NY + 1 :]
    to_team = lambda a: [a[0], shift(a[1], "y", 1), shift(a[2], "y", 2), shift(a[3], "y", -1)]
    spread = lambda a, axes, n: lax.all_to_all(jnp.broadcast_to(a[None], (n,) + a.shape), axes, 0, 0).reshape(-1, width)

    lead = to_team(lead)
    far = [shift(shift(main[2], "y", 1), "y", 1), shift(shift(main[4], "y", -1), "y", -1)]
    main = [main[0], shift(main[1], "y", 1), jnp.concatenate(far, 0), shift(main[3], "y", -1)]
    f_keep, f_send = join(place, lead, g_few)
    f_own, f_other = project(f_keep, shift(f_send, "c", 1), w_own, *w_other)
    rows = (hidden_few.astype(F32) + (f_own + shift(f_other, "c", 1).astype(F32))[:8]).astype(BF).astype(F32)
    normed = (rows * lax.rsqrt(jnp.mean(rows * rows, axis=-1, keepdims=True) + 1e-6) * norm_gain).astype(BF)
    per_z = spread(normed, "z", NZ)
    lag = conv_weight.shape[0] - 1
    rims = jnp.concatenate([resid[HALF - lag : HALF], resid[2 * HALF - lag :]], 0)
    per_z, rims, *main = lax.optimization_barrier((per_z, rims, *main))
    every = spread(per_z, ("y", "xl"), NY * NX)

    hidden = hidden_rows(resid, rims, conv_weight, me, NY * NZ * NX * NC - 1)
    keep, send = join(place, main, gates)
    p_own, p_other = project(keep, shift(send, "c", 1), w_own, *w_other)
    mixed = (hidden.astype(F32) + p_own + shift(p_other, "c", 1).astype(F32)).astype(BF)

    theirs = shift(every, "c", 1)
    who = c.astype(jnp.int32).reshape(1)
    logits = lens(who, every, lens_weight)
    logits = lens(1 - who, theirs, lens_weight, logits)
    return mixed, logits.reshape(-1, lens_weight.shape[1])


def solution(mesh):
    fine = Mesh(mesh.devices.reshape(NY, NZ, NX, NC, -1), ("y", "z", "xl", "c", "dp"))
    rows = P(("dp", "y", "z", "xl", "c"), None)
    return jax.shard_map(
        body,
        mesh=fine,
        in_specs=(rows, P(), rows, rows, rows, rows, P(("z", "xl", "c"), None), P(), P(None, ("y", "z", "xl", "c"))),
        out_specs=(rows, P("dp", ("y", "z", "xl", "c"))),
        check_vma=False,
    )
```

```python
import functools
import math

import jax
import jax.numpy as jnp
from jax import lax
from jax.experimental import pallas as pl
from jax.experimental.pallas import tpu as pltpu
from jax.sharding import Mesh
from jax.sharding import PartitionSpec as P

NY, NZ, NX, NC = 4, 8, 2, 2
HEADS, HD = 8, 256
HALF = 64
TEAM = NX * NC
SPAN = NZ * NX * NC * HALF
NEG = -1e30
BK, HB = 1024, 8
BF = jnp.bfloat16
F32 = jnp.float32


def packed(block):
    hi = block.astype(BF)
    rest = block - hi.astype(F32)
    mid = rest.astype(BF)
    low = (rest - mid.astype(F32)).astype(BF)
    pad = jnp.zeros((16 - block.shape[0], block.shape[1]), F32)
    return [jnp.concatenate([p.astype(F32), pad], 0).astype(BF) for p in (hi, mid, low)]


def attention_kernel(layout, place, *refs):
    n_kv = len(layout)
    q_refs, kv_refs, refs = refs[: NY + 1], refs[NY + 1 : NY + 1 + n_kv], refs[NY + 1 + n_kv :]
    outs, few_outs, refs = refs[: NY + 1], refs[NY + 1 : 2 * NY + 1], refs[2 * NY + 1 :]
    kvs, qs, acc, m_s, l_s, stage, ahead, sems = refs
    y, z, xl, c = place[0], place[1], place[2], place[3]
    copies = []

    def copy(src, dst):
        copies.append(pltpu.make_async_copy(src, dst, sems.at[len(copies)]))

    for ref, dy, halves in zip(q_refs, (0, 1, 3, 2, 2), ((0, 1), (0, 1), (0, 1), (0,), (1,))):
        for i, half in enumerate(halves):
            copy(ref.at[pl.ds(i * HALF, HALF)], qs.at[half * NY + ((y + dy) & (NY - 1))])
    for ref, entries in zip(kv_refs, layout):
        for at, (dz, dx, dc, r0, rows) in entries:
            s = (((z + dz) & (NZ - 1)) * NX + (xl ^ dx)) * NC + (c ^ dc)
            for half in range(2):
                low, high = max(r0, half * HALF), min(r0 + rows, (half + 1) * HALF)
                if low < high:
                    slot = (2 * NZ * NX * NC - 1 - s) if half else s
                    dst = kvs.at[pl.ds(pl.multiple_of(slot * HALF + low - half * HALF, 16), high - low)]
                    copy(ref.at[pl.ds(at + low - r0, high - low)], dst)
    for cp in copies:
        cp.start()
    m_s[...] = jnp.full_like(m_s, NEG)
    l_s[...] = jnp.zeros_like(l_s)
    acc[...] = jnp.zeros_like(acc)
    for cp in copies:
        cp.wait()

    qs[...] = qs[...] * BF(1.0 / math.sqrt(HD))
    tile = HB * HALF
    per = SPAN // BK
    me = (z * NX + xl) * NC + c
    early = me // (BK // HALF) + 1
    late = (NZ * NX * NC - 1 - me) // (BK // HALF) + 1
    n_whole = (2 * NY - 1) * per
    n_items = n_whole + early + late

    def place_of(i):
        e = i - NY * per
        f = e - (NY - 1 - y) * per
        p = i - n_whole
        g = jnp.where(e < 0, NY + i // per, jnp.where(f < 0, y + 1 + e // per, NY + f // per))
        kb = jnp.where(e < 0, i % per, jnp.where(f < 0, e % per, per + f % per))
        g = jnp.where(p < 0, g, jnp.where(p < early, y, NY + y))
        kb = jnp.where(p < 0, kb, jnp.where(p < early, p, per + p - early))
        return g, pl.multiple_of(kb * BK, BK)

    def scores(g, start, i):
        q = jnp.concatenate([qs[g, :, h * HD : (h + 1) * HD] for h in range(i * HB, (i + 1) * HB)], 0)
        return lax.dot_general(q, kvs[pl.ds(start, BK), :HD], (((1,), (1,)), ((), ())), preferred_element_type=F32)

    def fold(g, start, i, s, masked):
        rows = slice(i * tile, (i + 1) * tile)
        if masked:
            idx = start + lax.broadcasted_iota(jnp.int32, (HALF, BK), 1)
            k_pos = idx + jnp.where(idx < SPAN, y * SPAN, (2 * NY - 2 - y) * SPAN)
            row = lax.broadcasted_iota(jnp.int32, (HALF, BK), 0)
            st = (g & (NY - 1)) * (NZ * NX * NC) + me
            q_pos = jnp.where(g >= NY, 2 * NY * NZ * NX * NC - 1 - st, st) * HALF + row
            visible = k_pos <= q_pos
            s = jnp.concatenate([jnp.where(visible, s[h * HALF : (h + 1) * HALF], NEG) for h in range(HB)], 0)
        m_old = m_s[g, rows]
        mx = s[:, :128]
        for t in range(1, BK // 128):
            mx = jnp.maximum(mx, s[:, t * 128 : (t + 1) * 128])
        m_new = jnp.maximum(m_old, jnp.max(mx, axis=1, keepdims=True))
        alpha = jnp.exp(m_old - m_new)
        m_s[g, rows] = m_new
        parts, total = [], l_s[g, rows] * alpha
        for t in range(BK // 128):
            p = jnp.exp(s[:, t * 128 : (t + 1) * 128] - m_new)
            total = total + p
            parts.append(p.astype(BF))
        l_s[g, rows] = total
        v = kvs[pl.ds(start, BK), HD:]
        o = jnp.dot(jnp.concatenate(parts, 1), v, preferred_element_type=F32)
        acc[g, rows] = acc[g, rows] * jnp.concatenate([alpha, alpha], 1) + o

    def item(masked, i, carry):
        g, start = place_of(i)
        g_next, start_next = place_of(jnp.minimum(i + 1, n_items - 1))
        n = HEADS // HB
        s = ahead[...]
        for j in range(n):
            after = scores(g, start, j + 1) if j + 1 < n else scores(g_next, start_next, 0)
            fold(g, start, j, s, masked)
            s = after
        ahead[...] = s
        return carry

    ahead[...] = scores(*place_of(0), 0)
    lax.fori_loop(0, n_whole, functools.partial(item, False), 0)
    lax.fori_loop(n_whole, n_items, functools.partial(item, True), 0)

    lane = lax.broadcasted_iota(jnp.int32, (HALF, 128), 1)
    lane8 = lax.broadcasted_iota(jnp.int32, (8, 128), 1)
    pick = pl.ds(15, 4, stride=16)
    for dy in range(NY):
        lse = [jnp.zeros((HALF, 128), F32)] * 2
        few = jnp.zeros((8, 128), F32)
        for h in range(HEADS):
            rows = slice(h * HALF, (h + 1) * HALF)
            for half in range(2):
                g = half * NY + ((y + dy) & (NY - 1))
                total = jnp.maximum(jnp.sum(l_s[g, rows], axis=1, keepdims=True), 1e-30)
                value = m_s[g, rows] + jnp.log(total)
                lse[half] = jnp.where(lane == h, value, lse[half])
                o = acc[g, rows] * (1.0 / total)
                out, at = (outs[NY], 0) if dy == 2 and half else (outs[dy], half * HALF)
                out[at : at + HALF, h * HD : (h + 1) * HD] = o.astype(BF)
                stage[half * HALF : (half + 1) * HALF] = o[:, :128]
                stage[(2 + half) * HALF : (3 + half) * HALF] = o[:, 128:]
                stage[(4 + half) * HALF : (5 + half) * HALF] = value
            got = [stage[pl.ds(i * 2 * HALF + 15, 8, stride=16), :] for i in range(3)]
            few_outs[dy][:16, h * HD : (h + 1) * HD] = jnp.concatenate(
                [jnp.concatenate(got[:2], 1), jnp.zeros((8, HD), F32)], 0
            ).astype(BF)
            few = jnp.where(lane8 == h, got[2], few)
        block = jnp.concatenate(lse, 0).T[:HEADS]
        for out, blk, at in ((outs[NY], block, HALF) if dy == 2 else (outs[dy], block, 2 * HALF), (few_outs[dy], few, 16)):
            for p, v in enumerate(packed(blk)):
                out[at : at + 16, p * 128 : (p + 1) * 128] = v
            out[at : at + 16, 384:] = jnp.zeros((16, HEADS * HD - 384), BF)


def attention(place, qs, kv):
    tok, width = qs[0].shape
    layout = [e for _, e in kv]
    hbm = pl.BlockSpec(memory_space=pl.ANY)
    vm = pl.BlockSpec(memory_space=pltpu.VMEM)
    spans = [(r0, r0 + rows) for e in layout for _, (_, _, _, r0, rows) in e]
    n_copies = 2 * NY + sum(len([h for h in (0, 1) if max(a, h * HALF) < min(b, (h + 1) * HALF)]) for a, b in spans)
    return pl.pallas_call(
        functools.partial(attention_kernel, layout),
        in_specs=[pl.BlockSpec(memory_space=pltpu.SMEM)] + [hbm] * (len(qs) + len(kv)),
        out_specs=[vm] * (2 * NY + 1),
        out_shape=[jax.ShapeDtypeStruct((n, width), BF) for n in (tok + 16, tok + 16, HALF, tok + 16, HALF + 16)]
        + [jax.ShapeDtypeStruct((32, width), BF)] * NY,
        scratch_shapes=[
            pltpu.VMEM((2 * SPAN, 2 * HD), BF),
            pltpu.VMEM((2 * NY, HALF, width), BF),
            pltpu.VMEM((2 * NY, HEADS * HALF, HD), F32),
            pltpu.VMEM((2 * NY, HEADS * HALF, 128), F32),
            pltpu.VMEM((2 * NY, HEADS * HALF, 128), F32),
            pltpu.VMEM((6 * HALF, 128), F32),
            pltpu.VMEM((HB * HALF, BK), F32),
            pltpu.SemaphoreType.DMA((n_copies,)),
        ],
        compiler_params=pltpu.CompilerParams(vmem_limit_bytes=56 * 2**20),
        cost_estimate=pl.CostEstimate(flops=10**10, bytes_accessed=8 * 2**20, transcendentals=10**7),
    )(place, *qs, *[a for a, _ in kv])


def by_row(block, rows):
    if rows == 16:
        return jnp.concatenate([block, jnp.zeros((8, 128), F32)], 0)
    return jnp.concatenate([block, jnp.zeros((120, 128), F32)], 0).T


def join_kernel(rows, place, r0, r1, r2, r3, g_ref, keep_ref, send_ref):
    xl, c = place[2], place[3]
    refs = (r0, r1, r2, r3)
    blocks = []
    for r in refs:
        parts = [r[rows : rows + 16, p * 128 : (p + 1) * 128].astype(F32) for p in range(3)]
        blocks.append((parts[0] + parts[1] + parts[2])[:8])
    m = functools.reduce(jnp.maximum, blocks)
    exps = [jnp.exp(b - m) for b in blocks]
    total = exps[0] + exps[1] + exps[2] + exps[3]
    weights = [by_row(e / total, rows) for e in exps]
    low = lax.broadcasted_iota(jnp.int32, (rows, 128), 1) < 64
    for pair in range(HEADS // 2):
        quarters = []
        for h in (2 * pair, 2 * pair + 1):
            for t in range(2):
                cols = slice(h * HD + t * 128, h * HD + (t + 1) * 128)
                o = jnp.zeros((rows, 128), F32)
                for r, w in zip(refs, weights):
                    o = o + r[:rows, cols].astype(F32) * w[:, h : h + 1]
                quarters.append(jax.nn.sigmoid(g_ref[:, cols].astype(F32)) * o)
        cols = slice(pair * 128, (pair + 1) * 128)
        for t in range(2):
            a, b = quarters[t], quarters[2 + t]
            first = jnp.where(low, a, pltpu.roll(b, 64, 1))
            second = jnp.where(low, pltpu.roll(a, 64, 1), b)
            keep_ref[t ^ xl, :, cols] = jnp.where(c == 0, first, second).astype(BF)
            send_ref[t ^ xl, :, cols] = jnp.where(c == 0, second, first).astype(BF)


def join(place, parts, g):
    rows, width = g.shape
    vm = pl.BlockSpec(memory_space=pltpu.VMEM)
    half = jax.ShapeDtypeStruct((NX, rows, width // TEAM), BF)
    return pl.pallas_call(
        functools.partial(join_kernel, rows),
        in_specs=[pl.BlockSpec(memory_space=pltpu.SMEM)] + [vm] * 5,
        out_specs=[vm, vm],
        out_shape=[half, half],
        compiler_params=pltpu.CompilerParams(vmem_limit_bytes=24 * 2**20),
    )(place, *parts, g)


def project_kernel(rows, a_ref, b_ref, w0_hbm, w1_hbm, w2_hbm, keep_ref, send_ref, ws, sems):
    step = 512
    n = keep_ref.shape[1] // step
    loads = []
    for i in range(n):
        cols = slice(i * step, (i + 1) * step)
        at = 0
        for t, w in enumerate((w0_hbm, w1_hbm, w2_hbm)):
            n_rows = w.shape[0]
            loads.append(pltpu.make_async_copy(w.at[:, cols], ws.at[at : at + n_rows, cols], sems.at[i, t]))
            at += n_rows
    for load in loads:
        load.start()
    x = jnp.concatenate([jnp.concatenate([a_ref[t], b_ref[t]], 0) for t in range(NX)], 1)
    for i in range(n):
        for t in range(3):
            loads[3 * i + t].wait()
        cols = slice(i * step, (i + 1) * step)
        out = jnp.dot(x, ws[:, cols], preferred_element_type=F32)
        keep_ref[:, cols] = out[:rows]
        send_ref[:, cols] = out[rows:].astype(BF)


def project(a, b, w0, w1, w2):
    rows, width = a.shape[1], w0.shape[1]
    vm = pl.BlockSpec(memory_space=pltpu.VMEM)
    hbm = pl.BlockSpec(memory_space=pl.ANY)
    return pl.pallas_call(
        functools.partial(project_kernel, rows),
        in_specs=[vm, vm, hbm, hbm, hbm],
        out_specs=[vm, vm],
        out_shape=[jax.ShapeDtypeStruct((rows, width), F32), jax.ShapeDtypeStruct((rows, width), BF)],
        scratch_shapes=[pltpu.VMEM((NX * w0.shape[0], width), BF), pltpu.SemaphoreType.DMA((4, 3))],
        compiler_params=pltpu.CompilerParams(vmem_limit_bytes=24 * 2**20),
    )(a, b, w0, w1, w2)


def lens_kernel(who, x_ref, w_ref, *refs):
    out_ref = refs[-1]
    got = jnp.dot(x_ref[...], w_ref[...], preferred_element_type=F32)
    for i in range(out_ref.shape[0]):
        for j in range(NX):
            at = (i * NX + j) * NZ * 8
            out_ref[i, :, j, 0] = got[at : at + NZ * 8].reshape(NZ, 8, -1)


def lens(who, x, weight, before=None):
    ys = 2
    tile = ys * NX * NZ * 8
    rows, depth = x.shape
    vocab = weight.shape[1]
    extra = [] if before is None else [before]
    return pl.pallas_call(
        lens_kernel,
        grid_spec=pltpu.PrefetchScalarGridSpec(
            num_scalar_prefetch=1,
            grid=(rows // tile,),
            in_specs=[pl.BlockSpec((tile, depth), lambda i, w: (i, 0)), pl.BlockSpec((depth, vocab), lambda i, w: (0, 0))]
            + [pl.BlockSpec(memory_space=pl.ANY)] * len(extra),
            out_specs=pl.BlockSpec((ys, NZ, NX, 1, 8, vocab), lambda i, w: (i, 0, 0, w[0], 0, 0)),
        ),
        out_shape=jax.ShapeDtypeStruct((NY, NZ, NX, NC, 8, vocab), F32),
        input_output_aliases={} if before is None else {3: 0},
        compiler_params=pltpu.CompilerParams(vmem_limit_bytes=28 * 2**20),
        cost_estimate=pl.CostEstimate(flops=2 * rows * weight.size, bytes_accessed=6 * 2**20, transcendentals=0),
    )(who, x, weight, *extra)


def short_conv(prefix, rows, taps):
    lag = taps.shape[0] - 1
    extended = jnp.concatenate([prefix, rows], 0).astype(F32)
    total = jnp.zeros(rows.shape, F32)
    for t in range(lag + 1):
        total = total + taps[t].astype(F32) * extended[lag - t : lag - t + rows.shape[0]]
    return total


def hidden_rows(resid, rims, taps, me, last):
    lag = taps.shape[0] - 1
    count = NY * NZ * NX * NC
    names = ("y", "z", "xl", "c")
    low = lax.ppermute(rims[:lag], names, [(i, i + 1) for i in range(count - 1)])
    high = lax.ppermute(rims[lag:], names, [(i + 1, i) for i in range(count - 1)])
    high = jnp.where(me == last, resid[HALF - lag : HALF], high)
    conv = jnp.concatenate([short_conv(low, resid[:HALF], taps), short_conv(high, resid[HALF:], taps)], 0)
    return (resid.astype(F32) + jax.nn.silu(conv)).astype(BF)


def shift(x, axis, by):
    count = {"y": NY, "z": NZ, "xl": NX, "c": NC}[axis]
    return lax.ppermute(x, axis, [(i, (i + by) % count) for i in range(count)])


def body(resid, conv_weight, queries, keys, values, gates, out_weight, norm_gain, lens_weight):
    y, z, xl, c = (lax.axis_index(a) for a in ("y", "z", "xl", "c"))
    me = ((y * NZ + z) * NX + xl) * NC + c
    place = jnp.stack([y, z, xl, c]).astype(jnp.int32)
    tok, width = resid.shape
    few = lambda a: jnp.pad(a.reshape(8, 16, -1)[:, 15], ((0, 8), (0, 0)))

    w_own = lax.all_gather(out_weight, "z", axis=0, tiled=True)

    kv_own = lax.optimization_barrier(jnp.concatenate([keys, values], 1))
    q_up, q_down = shift(queries, "y", -1), shift(queries, "y", 1)
    q_far = [shift(q_down[:HALF], "y", 1), shift(q_up[HALF:], "y", -1)]
    pair = jnp.concatenate([kv_own, shift(kv_own, "xl", 1)], 0)
    both = lambda dz: [(dz, 0, 0, 0, tok), (dz, 1, 0, 0, tok)]
    held = [(pair, both(0))]
    fwd = bwd = pair
    for s in range(1, NZ // 2):
        fwd, bwd = shift(fwd, "z", 1), shift(bwd, "z", -1)
        if s < NZ // 2 - 1:
            held += [(fwd, both(-s)), (bwd, both(s))]
    taps = conv_weight.astype(F32)
    blocks = resid.reshape(8, 16, width)
    conv_few = sum(taps[t] * blocks[:, 15 - t].astype(F32) for t in range(conv_weight.shape[0]))
    hidden_few = (blocks[:, 15].astype(F32) + jax.nn.silu(conv_few)).astype(BF)
    g_few = few(gates)
    fwd, bwd, q_up, q_down, hidden_few, g_few, place, *q_far = lax.optimization_barrier(
        (fwd, bwd, q_up, q_down, hidden_few, g_few, place, *q_far)
    )
    held += [(fwd, both(1 - NZ // 2)), (bwd, both(NZ // 2 - 1))]
    held += [(shift(fwd[:tok], "z", 1), both(4)[:1]), (shift(bwd[tok:], "z", -1), both(4)[1:])]
    q_team = [queries, q_up, q_down] + q_far

    kv = []
    for group in (held[:7], held[7:]):
        entries, at = [], 0
        for piece, spans in group:
            kv.append((piece, [(i * tok, e) for i, e in enumerate(spans)]))
            for dz, dx, _, r0, n in spans:
                entries.append((at, (dz, dx, 1, r0, n)))
                at += n
        kv.append((shift(jnp.concatenate([p for p, _ in group], 0), "c", 1), entries))

    half_w = w_own.shape[0] // 2
    w_other = [
        shift(w_own[:half_w], "xl", 1),
        lax.ppermute(w_own[half_w:], ("xl", "dp"), [(i, 3 - i) for i in range(4)]),
    ]
    place, _ = lax.optimization_barrier((place, w_own))
    got = attention(place, q_team, kv)
    main, lead = got[: NY + 1], got[NY + 1 :]
    to_team = lambda a: [a[0], shift(a[1], "y", 1), shift(a[2], "y", 2), shift(a[3], "y", -1)]
    spread = lambda a, axes, n: lax.all_to_all(jnp.broadcast_to(a[None], (n,) + a.shape), axes, 0, 0).reshape(-1, width)

    lead = to_team(lead)
    f_keep, f_send = join(place, lead, g_few)
    f_own, f_other = project(f_keep, shift(f_send, "c", 1), w_own, *w_other)
    far = [shift(main[2], "y", 1), shift(main[4], "y", -1)]
    f_other = shift(f_other, "c", 1)
    lag = conv_weight.shape[0] - 1
    rims = jnp.concatenate([resid[HALF - lag : HALF], resid[2 * HALF - lag :]], 0)
    f_other, rims, *far = lax.optimization_barrier((f_other, rims, *far))
    far = [shift(far[0], "y", 1), shift(far[1], "y", -1)]
    near = [shift(main[1], "y", 1), shift(main[3], "y", -1)]
    rows = (hidden_few.astype(F32) + (f_own + f_other.astype(F32))[:8]).astype(BF).astype(F32)
    normed = (rows * lax.rsqrt(jnp.mean(rows * rows, axis=-1, keepdims=True) + 1e-6) * norm_gain).astype(BF)
    per_z = spread(normed, "z", NZ)
    per_z, *near = lax.optimization_barrier((per_z, *near))
    copies = jnp.broadcast_to(per_z[None], (NY * NX,) + per_z.shape)
    _, *far = lax.optimization_barrier((copies, *far))
    main = [main[0], near[0], jnp.concatenate(far, 0), near[1]]
    every = lax.all_to_all(copies, ("y", "xl"), 0, 0).reshape(-1, width)

    hidden = hidden_rows(resid, rims, conv_weight, me, NY * NZ * NX * NC - 1)
    keep, send = join(place, main, gates)
    p_own, p_other = project(keep, shift(send, "c", 1), w_own, *w_other)
    mixed = (hidden.astype(F32) + p_own + shift(p_other, "c", 1).astype(F32)).astype(BF)
    every, mixed = lax.optimization_barrier((every, mixed))

    theirs = shift(every, "c", 1)
    who = c.astype(jnp.int32).reshape(1)
    logits = lens(who, every, lens_weight)
    logits = lens(1 - who, theirs, lens_weight, logits)
    return mixed, logits.reshape(-1, lens_weight.shape[1])


def solution(mesh):
    fine = Mesh(mesh.devices.reshape(NY, NZ, NX, NC, -1), ("y", "z", "xl", "c", "dp"))
    rows = P(("dp", "y", "z", "xl", "c"), None)
    return jax.shard_map(
        body,
        mesh=fine,
        in_specs=(rows, P(), rows, rows, rows, rows, P(("z", "xl", "c"), None), P(), P(None, ("y", "z", "xl", "c"))),
        out_specs=(rows, P("dp", ("y", "z", "xl", "c"))),
        check_vma=False,
    )
```

```python
import functools
import math

import jax
import jax.numpy as jnp
from jax import lax
from jax.experimental import pallas as pl
from jax.experimental.pallas import tpu as pltpu
from jax.sharding import Mesh
from jax.sharding import PartitionSpec as P

NY, NZ, NX, NC = 4, 8, 2, 2
HEADS, HD = 8, 256
HALF = 64
TEAM = NX * NC
SPAN = NZ * NX * NC * HALF
NEG = -1e30
ORDER = (0, -1, 1, -2, 2, -3, 3, 4)
SWAP = 5
BK, HB = 1024, 8
BF = jnp.bfloat16
F32 = jnp.float32


def packed(block):
    hi = block.astype(BF)
    rest = block - hi.astype(F32)
    mid = rest.astype(BF)
    low = (rest - mid.astype(F32)).astype(BF)
    pad = jnp.zeros((16 - block.shape[0], block.shape[1]), F32)
    return [jnp.concatenate([p.astype(F32), pad], 0).astype(BF) for p in (hi, mid, low)]


def attention_kernel(layout, place, *refs):
    n_kv = len(layout)
    q_refs, kv_refs, refs = refs[: NY + 1], refs[NY + 1 : NY + 1 + n_kv], refs[NY + 1 + n_kv :]
    outs, few_outs, refs = refs[: NY + 1], refs[NY + 1 : 2 * NY + 1], refs[2 * NY + 1 :]
    kvs, qs, acc, m_s, l_s, stage, ahead, sems = refs
    y, z, xl, c = place[0], place[1], place[2], place[3]
    copies = []

    def copy(src, dst):
        copies.append(pltpu.make_async_copy(src, dst, sems.at[len(copies)]))

    for ref, dy, halves in zip(q_refs, (0, 1, 3, 2, 2), ((0, 1), (0, 1), (0, 1), (0,), (1,))):
        for i, half in enumerate(halves):
            copy(ref.at[pl.ds(i * HALF, HALF)], qs.at[half * NY + ((y + dy) & (NY - 1))])
    for ref, entries in zip(kv_refs, layout):
        for at, (dz, dx, dc, r0, rows) in entries:
            s = (((z + dz) & (NZ - 1)) * NX + (xl ^ dx)) * NC + (c ^ dc)
            for half in range(2):
                low, high = max(r0, half * HALF), min(r0 + rows, (half + 1) * HALF)
                if low < high:
                    slot = (2 * NZ * NX * NC - 1 - s) if half else s
                    dst = kvs.at[pl.ds(pl.multiple_of(slot * HALF + low - half * HALF, 16), high - low)]
                    copy(ref.at[pl.ds(at + low - r0, high - low)], dst)
    for cp in copies:
        cp.start()
    m_s[...] = jnp.full_like(m_s, NEG)
    l_s[...] = jnp.zeros_like(l_s)
    acc[...] = jnp.zeros_like(acc)
    for cp in copies:
        cp.wait()

    qs[...] = qs[...] * BF(1.0 / math.sqrt(HD))
    tile = HB * HALF
    per = SPAN // BK
    me = (z * NX + xl) * NC + c
    early = me // (BK // HALF) + 1
    late = (NZ * NX * NC - 1 - me) // (BK // HALF) + 1
    n_whole = (2 * NY - 1) * per
    n_items = n_whole + early + late

    def place_of(i):
        e = i - NY * per
        f = e - (NY - 1 - y) * per
        p = i - n_whole
        g = jnp.where(e < 0, NY + i // per, jnp.where(f < 0, y + 1 + e // per, NY + f // per))
        kb = jnp.where(e < 0, i % per, jnp.where(f < 0, e % per, per + f % per))
        g = jnp.where(p < 0, g, jnp.where(p < early, y, NY + y))
        kb = jnp.where(p < 0, kb, jnp.where(p < early, p, per + p - early))
        return g, pl.multiple_of(kb * BK, BK)

    def scores(g, start, i):
        q = jnp.concatenate([qs[g, :, h * HD : (h + 1) * HD] for h in range(i * HB, (i + 1) * HB)], 0)
        return lax.dot_general(q, kvs[pl.ds(start, BK), :HD], (((1,), (1,)), ((), ())), preferred_element_type=F32)

    def fold(g, start, i, s, masked):
        rows = slice(i * tile, (i + 1) * tile)
        if masked:
            idx = start + lax.broadcasted_iota(jnp.int32, (HALF, BK), 1)
            k_pos = idx + jnp.where(idx < SPAN, y * SPAN, (2 * NY - 2 - y) * SPAN)
            row = lax.broadcasted_iota(jnp.int32, (HALF, BK), 0)
            st = (g & (NY - 1)) * (NZ * NX * NC) + me
            q_pos = jnp.where(g >= NY, 2 * NY * NZ * NX * NC - 1 - st, st) * HALF + row
            visible = k_pos <= q_pos
            s = jnp.concatenate([jnp.where(visible, s[h * HALF : (h + 1) * HALF], NEG) for h in range(HB)], 0)
        m_old = m_s[g, rows]
        mx = s[:, :128]
        for t in range(1, BK // 128):
            mx = jnp.maximum(mx, s[:, t * 128 : (t + 1) * 128])
        m_new = jnp.maximum(m_old, jnp.max(mx, axis=1, keepdims=True))
        alpha = jnp.exp(m_old - m_new)
        m_s[g, rows] = m_new
        parts, total = [], l_s[g, rows] * alpha
        for t in range(BK // 128):
            p = jnp.exp(s[:, t * 128 : (t + 1) * 128] - m_new)
            total = total + p
            parts.append(p.astype(BF))
        l_s[g, rows] = total
        v = kvs[pl.ds(start, BK), HD:]
        o = jnp.dot(jnp.concatenate(parts, 1), v, preferred_element_type=F32)
        acc[g, rows] = acc[g, rows] * jnp.concatenate([alpha, alpha], 1) + o

    def item(masked, i, carry):
        g, start = place_of(i)
        g_next, start_next = place_of(jnp.minimum(i + 1, n_items - 1))
        n = HEADS // HB
        s = ahead[...]
        for j in range(n):
            after = scores(g, start, j + 1) if j + 1 < n else scores(g_next, start_next, 0)
            fold(g, start, j, s, masked)
            s = after
        ahead[...] = s
        return carry

    ahead[...] = scores(*place_of(0), 0)
    lax.fori_loop(0, n_whole, functools.partial(item, False), 0)
    lax.fori_loop(n_whole, n_items, functools.partial(item, True), 0)

    lane = lax.broadcasted_iota(jnp.int32, (HALF, 128), 1)
    lane8 = lax.broadcasted_iota(jnp.int32, (8, 128), 1)
    pick = pl.ds(15, 4, stride=16)
    for dy in range(NY):
        lse = [jnp.zeros((HALF, 128), F32)] * 2
        few = jnp.zeros((8, 128), F32)
        for h in range(HEADS):
            rows = slice(h * HALF, (h + 1) * HALF)
            for half in range(2):
                g = half * NY + ((y + dy) & (NY - 1))
                total = jnp.maximum(jnp.sum(l_s[g, rows], axis=1, keepdims=True), 1e-30)
                value = m_s[g, rows] + jnp.log(total)
                lse[half] = jnp.where(lane == h, value, lse[half])
                o = acc[g, rows] * (1.0 / total)
                out, at = (outs[NY], 0) if dy == 2 and half else (outs[dy], half * HALF)
                out[at : at + HALF, h * HD : (h + 1) * HD] = o.astype(BF)
                stage[half * HALF : (half + 1) * HALF] = o[:, :128]
                stage[(2 + half) * HALF : (3 + half) * HALF] = o[:, 128:]
                stage[(4 + half) * HALF : (5 + half) * HALF] = value
            got = [stage[pl.ds(i * 2 * HALF + 15, 8, stride=16), :] for i in range(3)]
            few_outs[dy][:16, h * HD : (h + 1) * HD] = jnp.concatenate(
                [jnp.concatenate(got[:2], 1), jnp.zeros((8, HD), F32)], 0
            ).astype(BF)
            few = jnp.where(lane8 == h, got[2], few)
        block = jnp.concatenate(lse, 0).T[:HEADS]
        for out, blk, at in ((outs[NY], block, HALF) if dy == 2 else (outs[dy], block, 2 * HALF), (few_outs[dy], few, 16)):
            for p, v in enumerate(packed(blk)):
                out[at : at + 16, p * 128 : (p + 1) * 128] = v
            out[at : at + 16, 384:] = jnp.zeros((16, HEADS * HD - 384), BF)


def attention(place, qs, kv):
    tok, width = qs[0].shape
    layout = [e for _, e in kv]
    hbm = pl.BlockSpec(memory_space=pl.ANY)
    vm = pl.BlockSpec(memory_space=pltpu.VMEM)
    spans = [(r0, r0 + rows) for e in layout for _, (_, _, _, r0, rows) in e]
    n_copies = 2 * NY + sum(len([h for h in (0, 1) if max(a, h * HALF) < min(b, (h + 1) * HALF)]) for a, b in spans)
    return pl.pallas_call(
        functools.partial(attention_kernel, layout),
        in_specs=[pl.BlockSpec(memory_space=pltpu.SMEM)] + [hbm] * (len(qs) + len(kv)),
        out_specs=[vm] * (2 * NY + 1),
        out_shape=[jax.ShapeDtypeStruct((n, width), BF) for n in (tok + 16, tok + 16, HALF, tok + 16, HALF + 16)]
        + [jax.ShapeDtypeStruct((32, width), BF)] * NY,
        scratch_shapes=[
            pltpu.VMEM((2 * SPAN, 2 * HD), BF),
            pltpu.VMEM((2 * NY, HALF, width), BF),
            pltpu.VMEM((2 * NY, HEADS * HALF, HD), F32),
            pltpu.VMEM((2 * NY, HEADS * HALF, 128), F32),
            pltpu.VMEM((2 * NY, HEADS * HALF, 128), F32),
            pltpu.VMEM((6 * HALF, 128), F32),
            pltpu.VMEM((HB * HALF, BK), F32),
            pltpu.SemaphoreType.DMA((n_copies,)),
        ],
        compiler_params=pltpu.CompilerParams(vmem_limit_bytes=56 * 2**20),
        cost_estimate=pl.CostEstimate(flops=10**10, bytes_accessed=8 * 2**20, transcendentals=10**7),
    )(place, *qs, *[a for a, _ in kv])


def by_row(block, rows):
    if rows == 16:
        return jnp.concatenate([block, jnp.zeros((8, 128), F32)], 0)
    return jnp.concatenate([block, jnp.zeros((120, 128), F32)], 0).T


def join_kernel(rows, place, r0, r1, r2, r3, g_ref, keep_ref, send_ref):
    xl, c = place[2], place[3]
    refs = (r0, r1, r2, r3)
    blocks = []
    for r in refs:
        parts = [r[rows : rows + 16, p * 128 : (p + 1) * 128].astype(F32) for p in range(3)]
        blocks.append((parts[0] + parts[1] + parts[2])[:8])
    m = functools.reduce(jnp.maximum, blocks)
    exps = [jnp.exp(b - m) for b in blocks]
    total = exps[0] + exps[1] + exps[2] + exps[3]
    weights = [by_row(e / total, rows) for e in exps]
    low = lax.broadcasted_iota(jnp.int32, (rows, 128), 1) < 64
    for pair in range(HEADS // 2):
        quarters = []
        for h in (2 * pair, 2 * pair + 1):
            for t in range(2):
                cols = slice(h * HD + t * 128, h * HD + (t + 1) * 128)
                o = jnp.zeros((rows, 128), F32)
                for r, w in zip(refs, weights):
                    o = o + r[:rows, cols].astype(F32) * w[:, h : h + 1]
                quarters.append(jax.nn.sigmoid(g_ref[:, cols].astype(F32)) * o)
        cols = slice(pair * 128, (pair + 1) * 128)
        for t in range(2):
            a, b = quarters[t], quarters[2 + t]
            first = jnp.where(low, a, pltpu.roll(b, 64, 1))
            second = jnp.where(low, pltpu.roll(a, 64, 1), b)
            keep_ref[t ^ xl, :, cols] = jnp.where(c == 0, first, second).astype(BF)
            send_ref[t ^ xl, :, cols] = jnp.where(c == 0, second, first).astype(BF)


def join(place, parts, g):
    rows, width = g.shape
    vm = pl.BlockSpec(memory_space=pltpu.VMEM)
    half = jax.ShapeDtypeStruct((NX, rows, width // TEAM), BF)
    return pl.pallas_call(
        functools.partial(join_kernel, rows),
        in_specs=[pl.BlockSpec(memory_space=pltpu.SMEM)] + [vm] * 5,
        out_specs=[vm, vm],
        out_shape=[half, half],
        compiler_params=pltpu.CompilerParams(vmem_limit_bytes=24 * 2**20),
    )(place, *parts, g)


def project_kernel(rows, parts, place, a_ref, b_ref, *refs):
    w_refs, (keep_ref, send_ref, ws, sems) = refs[: len(parts)], refs[len(parts) :]
    z, dp = place[1], place[4]
    loads = []
    for w, (part, flip, first) in zip(w_refs, parts):
        for i in range(w.shape[0]):
            head = (z + ORDER[first + i] + NZ) & (NZ - 1)
            row = part * HEADS * HALF + head * HALF + (dp ^ flip) * 32
            dst = ws.at[:, pl.ds(pl.multiple_of(row, 32), 32)]
            loads.append(pltpu.make_async_copy(w.at[i], dst, sems.at[len(loads)]))
    for load in loads:
        load.start()
    x = jnp.concatenate([jnp.concatenate([a_ref[t], b_ref[t]], 0) for t in range(NX)], 1)
    for load in loads:
        load.wait()
    step = ws.shape[2]
    for i in range(ws.shape[0]):
        cols = slice(i * step, (i + 1) * step)
        out = jnp.dot(x, ws[i], preferred_element_type=F32)
        keep_ref[:, cols] = out[:rows]
        send_ref[:, cols] = out[rows:].astype(BF)


def project(place, a, b, weights):
    rows = a.shape[1]
    _, groups, _, step = weights[0][0].shape
    width = groups * step
    vm = pl.BlockSpec(memory_space=pltpu.VMEM)
    hbm = pl.BlockSpec(memory_space=pl.ANY)
    n = sum(w.shape[0] for w, _ in weights)
    return pl.pallas_call(
        functools.partial(project_kernel, rows, [p for _, p in weights]),
        in_specs=[pl.BlockSpec(memory_space=pltpu.SMEM), vm, vm] + [hbm] * len(weights),
        out_specs=[vm, vm],
        out_shape=[jax.ShapeDtypeStruct((rows, width), F32), jax.ShapeDtypeStruct((rows, width), BF)],
        scratch_shapes=[pltpu.VMEM((groups, NX * HEADS * HALF, step), BF), pltpu.SemaphoreType.DMA((n,))],
        compiler_params=pltpu.CompilerParams(vmem_limit_bytes=24 * 2**20),
    )(place, a, b, *[w for w, _ in weights])


def lens_kernel(who, x_ref, w_ref, *refs):
    out_ref = refs[-1]
    got = jnp.dot(x_ref[...], w_ref[...], preferred_element_type=F32)
    for i in range(out_ref.shape[0]):
        for j in range(NX):
            at = (i * NX + j) * NZ * 8
            out_ref[i, :, j, 0] = got[at : at + NZ * 8].reshape(NZ, 8, -1)


def lens(who, x, weight, before=None):
    ys = 2
    tile = ys * NX * NZ * 8
    rows, depth = x.shape
    vocab = weight.shape[1]
    extra = [] if before is None else [before]
    return pl.pallas_call(
        lens_kernel,
        grid_spec=pltpu.PrefetchScalarGridSpec(
            num_scalar_prefetch=1,
            grid=(rows // tile,),
            in_specs=[pl.BlockSpec((tile, depth), lambda i, w: (i, 0)), pl.BlockSpec((depth, vocab), lambda i, w: (0, 0))]
            + [pl.BlockSpec(memory_space=pl.ANY)] * len(extra),
            out_specs=pl.BlockSpec((ys, NZ, NX, 1, 8, vocab), lambda i, w: (i, 0, 0, w[0], 0, 0)),
        ),
        out_shape=jax.ShapeDtypeStruct((NY, NZ, NX, NC, 8, vocab), F32),
        input_output_aliases={} if before is None else {3: 0},
        compiler_params=pltpu.CompilerParams(vmem_limit_bytes=28 * 2**20),
        cost_estimate=pl.CostEstimate(flops=2 * rows * weight.size, bytes_accessed=6 * 2**20, transcendentals=0),
    )(who, x, weight, *extra)


def short_conv(prefix, rows, taps):
    lag = taps.shape[0] - 1
    extended = jnp.concatenate([prefix, rows], 0).astype(F32)
    total = jnp.zeros(rows.shape, F32)
    for t in range(lag + 1):
        total = total + taps[t].astype(F32) * extended[lag - t : lag - t + rows.shape[0]]
    return total


def hidden_rows(resid, rims, taps, me, last):
    lag = taps.shape[0] - 1
    count = NY * NZ * NX * NC
    names = ("y", "z", "xl", "c")
    low = lax.ppermute(rims[:lag], names, [(i, i + 1) for i in range(count - 1)])
    high = lax.ppermute(rims[lag:], names, [(i + 1, i) for i in range(count - 1)])
    high = jnp.where(me == last, resid[HALF - lag : HALF], high)
    conv = jnp.concatenate([short_conv(low, resid[:HALF], taps), short_conv(high, resid[HALF:], taps)], 0)
    return (resid.astype(F32) + jax.nn.silu(conv)).astype(BF)


def shift(x, axis, by):
    count = {"y": NY, "z": NZ, "xl": NX, "c": NC}[axis]
    return lax.ppermute(x, axis, [(i, (i + by) % count) for i in range(count)])


def body(resid, conv_weight, queries, keys, values, gates, out_weight, norm_gain, lens_weight):
    y, z, xl, c = (lax.axis_index(a) for a in ("y", "z", "xl", "c"))
    me = ((y * NZ + z) * NX + xl) * NC + c
    dp = lax.axis_index("dp")
    place = jnp.stack([y, z, xl, c, dp]).astype(jnp.int32)
    tok, width = resid.shape
    few = lambda a: jnp.pad(a.reshape(8, 16, -1)[:, 15], ((0, 8), (0, 0)))

    w_half = jnp.where(dp == 0, out_weight[:32], out_weight[32:])
    w_block = jnp.concatenate([w_half[:, i * 512 : (i + 1) * 512] for i in range(width // 512)], 0)

    kv_own = lax.optimization_barrier(jnp.concatenate([keys, values], 1))
    q_up, q_down = shift(queries, "y", -1), shift(queries, "y", 1)
    q_far = [shift(q_down[:HALF], "y", 1), shift(q_up[HALF:], "y", -1)]
    load = jnp.concatenate([kv_own, shift(kv_own, "xl", 1), w_block], 0)
    n_kv, half = 2 * tok, load.shape[0] // 2
    both = lambda dz: [(0, (dz, 0, 0, 0, tok)), (tok, (dz, 1, 0, 0, tok))]
    held = [(load, n_kv, both(0))]
    fwd = bwd = load
    for s in range(1, NZ // 2):
        fwd, bwd = shift(fwd, "z", 1), shift(bwd, "z", -1)
        if s < NZ // 2 - 1:
            held += [(fwd, n_kv, both(-s)), (bwd, n_kv, both(s))]
    taps = conv_weight.astype(F32)
    blocks = resid.reshape(8, 16, width)
    conv_few = sum(taps[t] * blocks[:, 15 - t].astype(F32) for t in range(conv_weight.shape[0]))
    hidden_few = (blocks[:, 15].astype(F32) + jax.nn.silu(conv_few)).astype(BF)
    g_few = few(gates)
    fwd, bwd, q_up, q_down, hidden_few, g_few, place, *q_far = lax.optimization_barrier(
        (fwd, bwd, q_up, q_down, hidden_few, g_few, place, *q_far)
    )
    held += [(fwd, n_kv, both(1 - NZ // 2)), (bwd, n_kv, both(NZ // 2 - 1))]
    far_low, far_high = shift(fwd[:half], "z", 1), shift(bwd[half:], "z", -1)
    cut = half - tok
    held.append((far_low, half, [(0, (4, 0, 0, 0, tok)), (tok, (4, 1, 0, 0, cut))]))
    held.append((far_high, tok - cut, [(0, (4, 1, 0, cut, tok - cut))]))
    q_team = [queries, q_up, q_down] + q_far

    kv = []
    for group in (held[:SWAP], held[SWAP:]):
        entries, base = [], 0
        for piece, n, spans in group:
            kv.append((piece, spans))
            entries += [(base + at, (dz, dx, 1, r0, rows)) for at, (dz, dx, _, r0, rows) in spans]
            base += n
        kv.append((shift(jnp.concatenate([p[:n] for p, n, _ in group], 0), "c", 1), entries))

    shape = (NZ, width // 512, 32, 512)
    w_own = jnp.concatenate([p[n_kv:] for p, _, _ in held[:-2]] + [far_high[tok - cut :]], 0).reshape(shape)
    across = lambda a: lax.ppermute(a, ("xl", "dp"), [(i, 3 - i) for i in range(4)])
    w_x, w_d = shift(w_own, "xl", 1), across(w_own)
    place, _ = lax.optimization_barrier((place, w_own))
    got = attention(place, q_team, kv)
    main, lead = got[: NY + 1], got[NY + 1 :]
    to_team = lambda a: [a[0], shift(a[1], "y", 1), shift(a[2], "y", 2), shift(a[3], "y", -1)]
    spread = lambda a, axes, n: lax.all_to_all(jnp.broadcast_to(a[None], (n,) + a.shape), axes, 0, 0).reshape(-1, width)

    w_far = [across(w_x[: NZ // 2]), shift(w_d[NZ // 2 :], "xl", 1)]
    weights = [(w_own, (0, 0, 0)), (w_x, (1, 0, 0)), (w_d, (1, 1, 0))]
    weights += [(w_far[0], (0, 1, 0)), (w_far[1], (0, 1, NZ // 2))]
    lead = to_team(lead)
    f_keep, f_send = join(place, lead, g_few)
    f_own, f_other = project(place, f_keep, shift(f_send, "c", 1), weights)
    far = [shift(main[2], "y", 1), shift(main[4], "y", -1)]
    f_other = shift(f_other, "c", 1)
    lag = conv_weight.shape[0] - 1
    rims = jnp.concatenate([resid[HALF - lag : HALF], resid[2 * HALF - lag :]], 0)
    f_other, rims, *far = lax.optimization_barrier((f_other, rims, *far))
    far = [shift(far[0], "y", 1), shift(far[1], "y", -1)]
    near = [shift(main[1], "y", 1), shift(main[3], "y", -1)]
    rows = (hidden_few.astype(F32) + (f_own + f_other.astype(F32))[:8]).astype(BF).astype(F32)
    normed = (rows * lax.rsqrt(jnp.mean(rows * rows, axis=-1, keepdims=True) + 1e-6) * norm_gain).astype(BF)
    per_z = spread(normed, "z", NZ)
    per_z, *near = lax.optimization_barrier((per_z, *near))
    copies = jnp.broadcast_to(per_z[None], (NY * NX,) + per_z.shape)
    _, *far = lax.optimization_barrier((copies, *far))
    main = [main[0], near[0], jnp.concatenate(far, 0), near[1]]
    every = lax.all_to_all(copies, ("y", "xl"), 0, 0).reshape(-1, width)

    hidden = hidden_rows(resid, rims, conv_weight, me, NY * NZ * NX * NC - 1)
    keep, send = join(place, main, gates)
    p_own, p_other = project(place, keep, shift(send, "c", 1), weights)
    mixed = (hidden.astype(F32) + p_own + shift(p_other, "c", 1).astype(F32)).astype(BF)
    every, mixed = lax.optimization_barrier((every, mixed))

    theirs = shift(every, "c", 1)
    who = c.astype(jnp.int32).reshape(1)
    logits = lens(who, every, lens_weight)
    logits = lens(1 - who, theirs, lens_weight, logits)
    return mixed, logits.reshape(-1, lens_weight.shape[1])


def solution(mesh):
    fine = Mesh(mesh.devices.reshape(NY, NZ, NX, NC, -1), ("y", "z", "xl", "c", "dp"))
    rows = P(("dp", "y", "z", "xl", "c"), None)
    return jax.shard_map(
        body,
        mesh=fine,
        in_specs=(rows, P(), rows, rows, rows, rows, P(("z", "xl", "c"), None), P(), P(None, ("y", "z", "xl", "c"))),
        out_specs=(rows, P("dp", ("y", "z", "xl", "c"))),
        check_vma=False,
    )
```

```python
import functools
import math

import jax
import jax.numpy as jnp
from jax import lax
from jax.experimental import pallas as pl
from jax.experimental.pallas import tpu as pltpu
from jax.sharding import Mesh
from jax.sharding import PartitionSpec as P

NY, NZ, NX, NC = 4, 8, 2, 2
HEADS, HD = 8, 256
HALF = 64
TEAM = NX * NC
SPAN = NZ * NX * NC * HALF
NEG = -1e30
ORDER = (0, -1, 1, -2, 2, -3, 3, 4)
SWAP = 5
BK, HB = 1024, 8
BF = jnp.bfloat16
F32 = jnp.float32


def packed(block):
    hi = block.astype(BF)
    rest = block - hi.astype(F32)
    mid = rest.astype(BF)
    low = (rest - mid.astype(F32)).astype(BF)
    pad = jnp.zeros((16 - block.shape[0], block.shape[1]), F32)
    return [jnp.concatenate([p.astype(F32), pad], 0).astype(BF) for p in (hi, mid, low)]


def attention_kernel(layout, place, *refs):
    n_kv = len(layout)
    q_refs, kv_refs, refs = refs[: NY + 1], refs[NY + 1 : NY + 1 + n_kv], refs[NY + 1 + n_kv :]
    outs, few_outs, refs = refs[: NY + 1], refs[NY + 1 : 2 * NY + 1], refs[2 * NY + 1 :]
    kvs, qs, acc, m_s, l_s, stage, ahead, sems, out_sems = refs[:9]
    to_hbm = [pltpu.make_async_copy(v, o, out_sems.at[i]) for i, (v, o) in enumerate(zip(refs[9:], outs + few_outs))]
    outs, few_outs = refs[9 : NY + 10], refs[NY + 10 :]
    y, z, xl, c = place[0], place[1], place[2], place[3]
    first, second = [], []

    def copy(src, dst, to=first):
        to.append(pltpu.make_async_copy(src, dst, sems.at[len(first) + len(second)]))

    for ref, dy, halves in zip(q_refs, (0, 1, 3, 2, 2), ((0, 1), (0, 1), (0, 1), (0,), (1,))):
        for i, half in enumerate(halves):
            copy(ref.at[pl.ds(i * HALF, HALF)], qs.at[half * NY + ((y + dy) & (NY - 1))])
    for ref, entries in zip(kv_refs, layout):
        for at, (dz, dx, dc, r0, rows) in entries:
            s = (((z + dz) & (NZ - 1)) * NX + (xl ^ dx)) * NC + (c ^ dc)
            for half in range(2):
                low, high = max(r0, half * HALF), min(r0 + rows, (half + 1) * HALF)
                if low < high:
                    slot = (2 * NZ * NX * NC - 1 - s) if half else s
                    dst = kvs.at[pl.ds(pl.multiple_of(slot * HALF + low - half * HALF, 16), high - low)]
                    copy(ref.at[pl.ds(at + low - r0, high - low)], dst, second if half else first)
    for cp in first + second:
        cp.start()
    m_s[...] = jnp.full_like(m_s, NEG)
    l_s[...] = jnp.zeros_like(l_s)
    acc[...] = jnp.zeros_like(acc)
    for cp in first:
        cp.wait()

    qs[...] = qs[...] * BF(1.0 / math.sqrt(HD))
    tile = HB * HALF
    per = SPAN // BK
    me = (z * NX + xl) * NC + c
    early = me // (BK // HALF) + 1
    late = (NZ * NX * NC - 1 - me) // (BK // HALF) + 1
    n_whole = (2 * NY - 1) * per
    n_items = n_whole + early + late

    def place_of(i):
        e = i - NY * per
        f = e - (NY - 1 - y) * per
        p = i - n_whole
        g = jnp.where(e < 0, NY + i // per, jnp.where(f < 0, y + 1 + e // per, NY + f // per))
        kb = jnp.where(e < 0, i % per, jnp.where(f < 0, e % per, per + f % per))
        g = jnp.where(p < 0, g, jnp.where(p < early, y, NY + y))
        kb = jnp.where(p < 0, kb, jnp.where(p < early, p, per + p - early))
        return g, pl.multiple_of(kb * BK, BK)

    def scores(g, start, i):
        q = jnp.concatenate([qs[g, :, h * HD : (h + 1) * HD] for h in range(i * HB, (i + 1) * HB)], 0)
        return lax.dot_general(q, kvs[pl.ds(start, BK), :HD], (((1,), (1,)), ((), ())), preferred_element_type=F32)

    def fold(g, start, i, s, masked):
        rows = slice(i * tile, (i + 1) * tile)
        if masked:
            idx = start + lax.broadcasted_iota(jnp.int32, (HALF, BK), 1)
            k_pos = idx + jnp.where(idx < SPAN, y * SPAN, (2 * NY - 2 - y) * SPAN)
            row = lax.broadcasted_iota(jnp.int32, (HALF, BK), 0)
            st = (g & (NY - 1)) * (NZ * NX * NC) + me
            q_pos = jnp.where(g >= NY, 2 * NY * NZ * NX * NC - 1 - st, st) * HALF + row
            visible = k_pos <= q_pos
            s = jnp.concatenate([jnp.where(visible, s[h * HALF : (h + 1) * HALF], NEG) for h in range(HB)], 0)
        m_old = m_s[g, rows]
        mx = s[:, :128]
        for t in range(1, BK // 128):
            mx = jnp.maximum(mx, s[:, t * 128 : (t + 1) * 128])
        m_new = jnp.maximum(m_old, jnp.max(mx, axis=1, keepdims=True))
        alpha = jnp.exp(m_old - m_new)
        m_s[g, rows] = m_new
        parts, total = [], l_s[g, rows] * alpha
        for t in range(BK // 128):
            p = jnp.exp(s[:, t * 128 : (t + 1) * 128] - m_new)
            total = total + p
            parts.append(p.astype(BF))
        l_s[g, rows] = total
        v = kvs[pl.ds(start, BK), HD:]
        o = jnp.dot(jnp.concatenate(parts, 1), v, preferred_element_type=F32)
        acc[g, rows] = acc[g, rows] * jnp.concatenate([alpha, alpha], 1) + o

    def item(masked, i, carry):
        g, start = place_of(i)
        g_next, start_next = place_of(jnp.minimum(i + 1, n_items - 1))
        n = HEADS // HB
        s = ahead[...]
        for j in range(n):
            after = scores(g, start, j + 1) if j + 1 < n else scores(g_next, start_next, 0)
            fold(g, start, j, s, masked)
            s = after
        ahead[...] = s
        return carry

    ahead[...] = scores(*place_of(0), 0)
    lax.fori_loop(0, NY * per - 1, functools.partial(item, False), 0)
    for cp in second:
        cp.wait()
    lax.fori_loop(NY * per - 1, n_whole, functools.partial(item, False), 0)
    lax.fori_loop(n_whole, n_items, functools.partial(item, True), 0)

    lane = lax.broadcasted_iota(jnp.int32, (HALF, 128), 1)
    lane8 = lax.broadcasted_iota(jnp.int32, (8, 128), 1)
    pick = pl.ds(15, 4, stride=16)
    for dy in range(NY):
        lse = [jnp.zeros((HALF, 128), F32)] * 2
        few = jnp.zeros((8, 128), F32)
        for h in range(HEADS):
            rows = slice(h * HALF, (h + 1) * HALF)
            for half in range(2):
                g = half * NY + ((y + dy) & (NY - 1))
                total = jnp.maximum(jnp.sum(l_s[g, rows], axis=1, keepdims=True), 1e-30)
                value = m_s[g, rows] + jnp.log(total)
                lse[half] = jnp.where(lane == h, value, lse[half])
                o = acc[g, rows] * (1.0 / total)
                out, at = (outs[NY], 0) if dy == 2 and half else (outs[dy], half * HALF)
                out[at : at + HALF, h * HD : (h + 1) * HD] = o.astype(BF)
                stage[half * HALF : (half + 1) * HALF] = o[:, :128]
                stage[(2 + half) * HALF : (3 + half) * HALF] = o[:, 128:]
                stage[(4 + half) * HALF : (5 + half) * HALF] = value
            got = [stage[pl.ds(i * 2 * HALF + 15, 8, stride=16), :] for i in range(3)]
            few_outs[dy][:16, h * HD : (h + 1) * HD] = jnp.concatenate(
                [jnp.concatenate(got[:2], 1), jnp.zeros((8, HD), F32)], 0
            ).astype(BF)
            few = jnp.where(lane8 == h, got[2], few)
        block = jnp.concatenate(lse, 0).T[:HEADS]
        for out, blk, at in ((outs[NY], block, HALF) if dy == 2 else (outs[dy], block, 2 * HALF), (few_outs[dy], few, 16)):
            for p, v in enumerate(packed(blk)):
                out[at : at + 16, p * 128 : (p + 1) * 128] = v
            out[at : at + 16, 384:] = jnp.zeros((16, HEADS * HD - 384), BF)
        for i in (dy, NY + 1 + dy) + ((NY,) if dy == 2 else ()):
            to_hbm[i].start()
    for cp in to_hbm:
        cp.wait()


def attention(place, qs, kv):
    tok, width = qs[0].shape
    layout = [e for _, e in kv]
    hbm = pl.BlockSpec(memory_space=pl.ANY)
    spans = [(r0, r0 + rows) for e in layout for _, (_, _, _, r0, rows) in e]
    n_copies = 2 * NY + sum(len([h for h in (0, 1) if max(a, h * HALF) < min(b, (h + 1) * HALF)]) for a, b in spans)
    shapes = [jax.ShapeDtypeStruct((n, width), BF) for n in (tok + 16, tok + 16, HALF, tok + 16, HALF + 16)]
    shapes += [jax.ShapeDtypeStruct((32, width), BF)] * NY
    return pl.pallas_call(
        functools.partial(attention_kernel, layout),
        in_specs=[pl.BlockSpec(memory_space=pltpu.SMEM)] + [hbm] * (len(qs) + len(kv)),
        out_specs=[hbm] * len(shapes),
        out_shape=shapes,
        scratch_shapes=[
            pltpu.VMEM((2 * SPAN, 2 * HD), BF),
            pltpu.VMEM((2 * NY, HALF, width), BF),
            pltpu.VMEM((2 * NY, HEADS * HALF, HD), F32),
            pltpu.VMEM((2 * NY, HEADS * HALF, 128), F32),
            pltpu.VMEM((2 * NY, HEADS * HALF, 128), F32),
            pltpu.VMEM((6 * HALF, 128), F32),
            pltpu.VMEM((HB * HALF, BK), F32),
            pltpu.SemaphoreType.DMA((n_copies,)),
            pltpu.SemaphoreType.DMA((len(shapes),)),
        ]
        + [pltpu.VMEM(o.shape, BF) for o in shapes],
        compiler_params=pltpu.CompilerParams(vmem_limit_bytes=56 * 2**20),
        cost_estimate=pl.CostEstimate(flops=10**10, bytes_accessed=8 * 2**20, transcendentals=10**7),
    )(place, *qs, *[a for a, _ in kv])


def by_row(block, rows):
    if rows == 16:
        return jnp.concatenate([block, jnp.zeros((8, 128), F32)], 0)
    return jnp.concatenate([block, jnp.zeros((120, 128), F32)], 0).T


def join_kernel(rows, place, r0, r1, r2, r3, g_ref, keep_ref, send_ref):
    xl, c = place[2], place[3]
    refs = (r0, r1, r2, r3)
    blocks = []
    for r in refs:
        parts = [r[rows : rows + 16, p * 128 : (p + 1) * 128].astype(F32) for p in range(3)]
        blocks.append((parts[0] + parts[1] + parts[2])[:8])
    m = functools.reduce(jnp.maximum, blocks)
    exps = [jnp.exp(b - m) for b in blocks]
    total = exps[0] + exps[1] + exps[2] + exps[3]
    weights = [by_row(e / total, rows) for e in exps]
    low = lax.broadcasted_iota(jnp.int32, (rows, 128), 1) < 64
    for pair in range(HEADS // 2):
        quarters = []
        for h in (2 * pair, 2 * pair + 1):
            for t in range(2):
                cols = slice(h * HD + t * 128, h * HD + (t + 1) * 128)
                o = jnp.zeros((rows, 128), F32)
                for r, w in zip(refs, weights):
                    o = o + r[:rows, cols].astype(F32) * w[:, h : h + 1]
                quarters.append(jax.nn.sigmoid(g_ref[:, cols].astype(F32)) * o)
        cols = slice(pair * 128, (pair + 1) * 128)
        for t in range(2):
            a, b = quarters[t], quarters[2 + t]
            first = jnp.where(low, a, pltpu.roll(b, 64, 1))
            second = jnp.where(low, pltpu.roll(a, 64, 1), b)
            keep_ref[t ^ xl, :, cols] = jnp.where(c == 0, first, second).astype(BF)
            send_ref[t ^ xl, :, cols] = jnp.where(c == 0, second, first).astype(BF)


def join(place, parts, g):
    rows, width = g.shape
    vm = pl.BlockSpec(memory_space=pltpu.VMEM)
    half = jax.ShapeDtypeStruct((NX, rows, width // TEAM), BF)
    return pl.pallas_call(
        functools.partial(join_kernel, rows),
        in_specs=[pl.BlockSpec(memory_space=pltpu.SMEM)] + [vm] * 5,
        out_specs=[vm, vm],
        out_shape=[half, half],
        compiler_params=pltpu.CompilerParams(vmem_limit_bytes=24 * 2**20),
    )(place, *parts, g)


def project_kernel(rows, parts, place, a_ref, b_ref, *refs):
    w_refs, (keep_ref, send_ref, ws, sems) = refs[: len(parts)], refs[len(parts) :]
    z, dp = place[1], place[4]
    loads = []
    for w, (part, flip, first) in zip(w_refs, parts):
        for i in range(w.shape[0]):
            head = (z + ORDER[first + i] + NZ) & (NZ - 1)
            row = part * HEADS * HALF + head * HALF + (dp ^ flip) * 32
            dst = ws.at[:, pl.ds(pl.multiple_of(row, 32), 32)]
            loads.append(pltpu.make_async_copy(w.at[i], dst, sems.at[len(loads)]))
    for load in loads:
        load.start()
    x = jnp.concatenate([jnp.concatenate([a_ref[t], b_ref[t]], 0) for t in range(NX)], 1)
    for load in loads:
        load.wait()
    step = ws.shape[2]
    for i in range(ws.shape[0]):
        cols = slice(i * step, (i + 1) * step)
        out = jnp.dot(x, ws[i], preferred_element_type=F32)
        keep_ref[:, cols] = out[:rows]
        send_ref[:, cols] = out[rows:].astype(BF)


def project(place, a, b, weights):
    rows = a.shape[1]
    _, groups, _, step = weights[0][0].shape
    width = groups * step
    vm = pl.BlockSpec(memory_space=pltpu.VMEM)
    hbm = pl.BlockSpec(memory_space=pl.ANY)
    n = sum(w.shape[0] for w, _ in weights)
    return pl.pallas_call(
        functools.partial(project_kernel, rows, [p for _, p in weights]),
        in_specs=[pl.BlockSpec(memory_space=pltpu.SMEM), vm, vm] + [hbm] * len(weights),
        out_specs=[vm, vm],
        out_shape=[jax.ShapeDtypeStruct((rows, width), F32), jax.ShapeDtypeStruct((rows, width), BF)],
        scratch_shapes=[pltpu.VMEM((groups, NX * HEADS * HALF, step), BF), pltpu.SemaphoreType.DMA((n,))],
        compiler_params=pltpu.CompilerParams(vmem_limit_bytes=24 * 2**20),
    )(place, a, b, *[w for w, _ in weights])


def lens_kernel(who, x_ref, w_ref, *refs):
    out_ref = refs[-1]
    got = jnp.dot(x_ref[...], w_ref[...], preferred_element_type=F32)
    for i in range(out_ref.shape[0]):
        for j in range(NX):
            at = (i * NX + j) * NZ * 8
            out_ref[i, :, j, 0] = got[at : at + NZ * 8].reshape(NZ, 8, -1)


def lens(who, x, weight, before=None):
    ys = 2
    tile = ys * NX * NZ * 8
    rows, depth = x.shape
    vocab = weight.shape[1]
    extra = [] if before is None else [before]
    return pl.pallas_call(
        lens_kernel,
        grid_spec=pltpu.PrefetchScalarGridSpec(
            num_scalar_prefetch=1,
            grid=(rows // tile,),
            in_specs=[pl.BlockSpec((tile, depth), lambda i, w: (i, 0)), pl.BlockSpec((depth, vocab), lambda i, w: (0, 0))]
            + [pl.BlockSpec(memory_space=pl.ANY)] * len(extra),
            out_specs=pl.BlockSpec((ys, NZ, NX, 1, 8, vocab), lambda i, w: (i, 0, 0, w[0], 0, 0)),
        ),
        out_shape=jax.ShapeDtypeStruct((NY, NZ, NX, NC, 8, vocab), F32),
        input_output_aliases={} if before is None else {3: 0},
        compiler_params=pltpu.CompilerParams(vmem_limit_bytes=28 * 2**20),
        cost_estimate=pl.CostEstimate(flops=2 * rows * weight.size, bytes_accessed=6 * 2**20, transcendentals=0),
    )(who, x, weight, *extra)


def short_conv(prefix, rows, taps):
    lag = taps.shape[0] - 1
    extended = jnp.concatenate([prefix, rows], 0).astype(F32)
    total = jnp.zeros(rows.shape, F32)
    for t in range(lag + 1):
        total = total + taps[t].astype(F32) * extended[lag - t : lag - t + rows.shape[0]]
    return total


def hidden_rows(resid, rims, taps, me, last):
    lag = taps.shape[0] - 1
    count = NY * NZ * NX * NC
    names = ("y", "z", "xl", "c")
    low = lax.ppermute(rims[:lag], names, [(i, i + 1) for i in range(count - 1)])
    high = lax.ppermute(rims[lag:], names, [(i + 1, i) for i in range(count - 1)])
    high = jnp.where(me == last, resid[HALF - lag : HALF], high)
    conv = jnp.concatenate([short_conv(low, resid[:HALF], taps), short_conv(high, resid[HALF:], taps)], 0)
    return (resid.astype(F32) + jax.nn.silu(conv)).astype(BF)


def shift(x, axis, by):
    count = {"y": NY, "z": NZ, "xl": NX, "c": NC}[axis]
    return lax.ppermute(x, axis, [(i, (i + by) % count) for i in range(count)])


def body(resid, conv_weight, queries, keys, values, gates, out_weight, norm_gain, lens_weight):
    y, z, xl, c = (lax.axis_index(a) for a in ("y", "z", "xl", "c"))
    me = ((y * NZ + z) * NX + xl) * NC + c
    dp = lax.axis_index("dp")
    place = jnp.stack([y, z, xl, c, dp]).astype(jnp.int32)
    tok, width = resid.shape
    few = lambda a: jnp.pad(a.reshape(8, 16, -1)[:, 15], ((0, 8), (0, 0)))

    w_half = jnp.where(dp == 0, out_weight[:32], out_weight[32:])
    w_block = jnp.concatenate([w_half[:, i * 512 : (i + 1) * 512] for i in range(width // 512)], 0)

    kv_own = lax.optimization_barrier(jnp.concatenate([keys, values], 1))
    q_up, q_down = shift(queries, "y", -1), shift(queries, "y", 1)
    q_far = [shift(q_down[:HALF], "y", 1), shift(q_up[HALF:], "y", -1)]
    load = jnp.concatenate([kv_own, shift(kv_own, "xl", 1), w_block], 0)
    n_kv, half = 2 * tok, load.shape[0] // 2
    both = lambda dz: [(0, (dz, 0, 0, 0, tok)), (tok, (dz, 1, 0, 0, tok))]
    held = [(load, n_kv, both(0))]
    fwd = bwd = load
    for s in range(1, NZ // 2):
        fwd, bwd = shift(fwd, "z", 1), shift(bwd, "z", -1)
        if s < NZ // 2 - 1:
            held += [(fwd, n_kv, both(-s)), (bwd, n_kv, both(s))]
    taps = conv_weight.astype(F32)
    blocks = resid.reshape(8, 16, width)
    conv_few = sum(taps[t] * blocks[:, 15 - t].astype(F32) for t in range(conv_weight.shape[0]))
    hidden_few = (blocks[:, 15].astype(F32) + jax.nn.silu(conv_few)).astype(BF)
    g_few = few(gates)
    fwd, bwd, q_up, q_down, hidden_few, g_few, place, *q_far = lax.optimization_barrier(
        (fwd, bwd, q_up, q_down, hidden_few, g_few, place, *q_far)
    )
    held += [(fwd, n_kv, both(1 - NZ // 2)), (bwd, n_kv, both(NZ // 2 - 1))]
    far_low, far_high = shift(fwd[:half], "z", 1), shift(bwd[half:], "z", -1)
    cut = half - tok
    held.append((far_low, half, [(0, (4, 0, 0, 0, tok)), (tok, (4, 1, 0, 0, cut))]))
    held.append((far_high, tok - cut, [(0, (4, 1, 0, cut, tok - cut))]))
    q_team = [queries, q_up, q_down] + q_far

    kv = []
    for group in (held[:SWAP], held[SWAP:]):
        entries, base = [], 0
        for piece, n, spans in group:
            kv.append((piece, spans))
            entries += [(base + at, (dz, dx, 1, r0, rows)) for at, (dz, dx, _, r0, rows) in spans]
            base += n
        kv.append((shift(jnp.concatenate([p[:n] for p, n, _ in group], 0), "c", 1), entries))

    shape = (NZ, width // 512, 32, 512)
    w_own = jnp.concatenate([p[n_kv:] for p, _, _ in held[:-2]] + [far_high[tok - cut :]], 0).reshape(shape)
    across = lambda a: lax.ppermute(a, ("xl", "dp"), [(i, 3 - i) for i in range(4)])
    w_x, w_d = shift(w_own, "xl", 1), across(w_own)
    place, _ = lax.optimization_barrier((place, w_own))
    got = attention(place, q_team, kv)
    main, lead = got[: NY + 1], got[NY + 1 :]
    to_team = lambda a: [a[0], shift(a[1], "y", 1), shift(a[2], "y", 2), shift(a[3], "y", -1)]
    spread = lambda a, axes, n: lax.all_to_all(jnp.broadcast_to(a[None], (n,) + a.shape), axes, 0, 0).reshape(-1, width)

    w_far = [across(w_x[: NZ // 2]), shift(w_d[NZ // 2 :], "xl", 1)]
    weights = [(w_own, (0, 0, 0)), (w_x, (1, 0, 0)), (w_d, (1, 1, 0))]
    weights += [(w_far[0], (0, 1, 0)), (w_far[1], (0, 1, NZ // 2))]
    lead = to_team(lead)
    f_keep, f_send = join(place, lead, g_few)
    f_own, f_other = project(place, f_keep, shift(f_send, "c", 1), weights)
    far = [shift(main[2], "y", 1), shift(main[4], "y", -1)]
    f_other = shift(f_other, "c", 1)
    lag = conv_weight.shape[0] - 1
    rims = jnp.concatenate([resid[HALF - lag : HALF], resid[2 * HALF - lag :]], 0)
    f_other, rims, *far = lax.optimization_barrier((f_other, rims, *far))
    far = [shift(far[0], "y", 1), shift(far[1], "y", -1)]
    near = [shift(main[1], "y", 1), shift(main[3], "y", -1)]
    rows = (hidden_few.astype(F32) + (f_own + f_other.astype(F32))[:8]).astype(BF).astype(F32)
    normed = (rows * lax.rsqrt(jnp.mean(rows * rows, axis=-1, keepdims=True) + 1e-6) * norm_gain).astype(BF)
    per_z = spread(normed, "z", NZ)
    per_z, *near = lax.optimization_barrier((per_z, *near))
    copies = jnp.broadcast_to(per_z[None], (NY * NX,) + per_z.shape)
    _, *far = lax.optimization_barrier((copies, *far))
    main = [main[0], near[0], jnp.concatenate(far, 0), near[1]]
    every = lax.all_to_all(copies, ("y", "xl"), 0, 0).reshape(-1, width)

    hidden = hidden_rows(resid, rims, conv_weight, me, NY * NZ * NX * NC - 1)
    keep, send = join(place, main, gates)
    p_own, p_other = project(place, keep, shift(send, "c", 1), weights)
    mixed = (hidden.astype(F32) + p_own + shift(p_other, "c", 1).astype(F32)).astype(BF)
    every, mixed = lax.optimization_barrier((every, mixed))

    theirs = shift(every, "c", 1)
    who = c.astype(jnp.int32).reshape(1)
    logits = lens(who, every, lens_weight)
    logits = lens(1 - who, theirs, lens_weight, logits)
    return mixed, logits.reshape(-1, lens_weight.shape[1])


def solution(mesh):
    fine = Mesh(mesh.devices.reshape(NY, NZ, NX, NC, -1), ("y", "z", "xl", "c", "dp"))
    rows = P(("dp", "y", "z", "xl", "c"), None)
    return jax.shard_map(
        body,
        mesh=fine,
        in_specs=(rows, P(), rows, rows, rows, rows, P(("z", "xl", "c"), None), P(), P(None, ("y", "z", "xl", "c"))),
        out_specs=(rows, P("dp", ("y", "z", "xl", "c"))),
        check_vma=False,
    )
```

```python
import functools
import math

import jax
import jax.numpy as jnp
from jax import lax
from jax.experimental import pallas as pl
from jax.experimental.pallas import tpu as pltpu
from jax.sharding import Mesh
from jax.sharding import PartitionSpec as P

NY, NZ, NX, NC = 4, 8, 2, 2
HEADS, HD = 8, 256
HALF = 64
TEAM = NX * NC
SPAN = NZ * NX * NC * HALF
NEG = -1e30
ORDER = (0, -1, 1, -2, 2, -3, 3, 4)
SWAP = 5
BK, HB = 1024, 8
BF = jnp.bfloat16
F32 = jnp.float32


def packed(block):
    hi = block.astype(BF)
    rest = block - hi.astype(F32)
    mid = rest.astype(BF)
    low = (rest - mid.astype(F32)).astype(BF)
    pad = jnp.zeros((16 - block.shape[0], block.shape[1]), F32)
    return [jnp.concatenate([p.astype(F32), pad], 0).astype(BF) for p in (hi, mid, low)]


def attention_kernel(layout, place, *refs):
    n_kv = len(layout)
    q_refs, kv_refs, refs = refs[: NY + 1], refs[NY + 1 : NY + 1 + n_kv], refs[NY + 1 + n_kv :]
    outs, few_outs, refs = refs[: NY + 1], refs[NY + 1 : 2 * NY + 1], refs[2 * NY + 1 :]
    kvs, qs, acc, m_s, l_s, stage, ahead, sems, out_sems = refs[:9]
    to_hbm = [pltpu.make_async_copy(v, o, out_sems.at[i]) for i, (v, o) in enumerate(zip(refs[9:], outs + few_outs))]
    outs, few_outs = refs[9 : NY + 10], refs[NY + 10 :]
    y, z, xl, c = place[0], place[1], place[2], place[3]
    first, second = [], []

    def copy(src, dst, to=first):
        to.append(pltpu.make_async_copy(src, dst, sems.at[len(first) + len(second)]))

    for ref, dy, halves in zip(q_refs, (0, 1, 3, 2, 2), ((0, 1), (0, 1), (0, 1), (0,), (1,))):
        for i, half in enumerate(halves):
            copy(ref.at[pl.ds(i * HALF, HALF)], qs.at[half * NY + ((y + dy) & (NY - 1))])
    for ref, entries in zip(kv_refs, layout):
        for at, (dz, dx, dc, r0, rows) in entries:
            s = (((z + dz) & (NZ - 1)) * NX + (xl ^ dx)) * NC + (c ^ dc)
            for half in range(2):
                low, high = max(r0, half * HALF), min(r0 + rows, (half + 1) * HALF)
                if low < high:
                    slot = (2 * NZ * NX * NC - 1 - s) if half else s
                    dst = kvs.at[pl.ds(pl.multiple_of(slot * HALF + low - half * HALF, 16), high - low)]
                    copy(ref.at[pl.ds(at + low - r0, high - low)], dst, second if half else first)
    for cp in first + second:
        cp.start()
    m_s[...] = jnp.full_like(m_s, NEG)
    l_s[...] = jnp.zeros_like(l_s)
    acc[...] = jnp.zeros_like(acc)
    for cp in first:
        cp.wait()

    qs[...] = qs[...] * BF(1.0 / math.sqrt(HD))
    tile = HB * HALF
    per = SPAN // BK
    me = (z * NX + xl) * NC + c
    early = me // (BK // HALF) + 1
    late = (NZ * NX * NC - 1 - me) // (BK // HALF) + 1
    n_whole = (2 * NY - 1) * per
    n_items = n_whole + early + late

    def place_of(i):
        e = i - NY * per
        f = e - (NY - 1 - y) * per
        p = i - n_whole
        g = jnp.where(e < 0, NY + i // per, jnp.where(f < 0, y + 1 + e // per, NY + f // per))
        kb = jnp.where(e < 0, i % per, jnp.where(f < 0, e % per, per + f % per))
        g = jnp.where(p < 0, g, jnp.where(p < early, y, NY + y))
        kb = jnp.where(p < 0, kb, jnp.where(p < early, p, per + p - early))
        return g, pl.multiple_of(kb * BK, BK)

    def scores(g, start, i):
        q = jnp.concatenate([qs[g, :, h * HD : (h + 1) * HD] for h in range(i * HB, (i + 1) * HB)], 0)
        return lax.dot_general(q, kvs[pl.ds(start, BK), :HD], (((1,), (1,)), ((), ())), preferred_element_type=F32)

    def fold(g, start, i, s, masked):
        rows = slice(i * tile, (i + 1) * tile)
        if masked:
            idx = start + lax.broadcasted_iota(jnp.int32, (HALF, BK), 1)
            k_pos = idx + jnp.where(idx < SPAN, y * SPAN, (2 * NY - 2 - y) * SPAN)
            row = lax.broadcasted_iota(jnp.int32, (HALF, BK), 0)
            st = (g & (NY - 1)) * (NZ * NX * NC) + me
            q_pos = jnp.where(g >= NY, 2 * NY * NZ * NX * NC - 1 - st, st) * HALF + row
            visible = k_pos <= q_pos
            s = jnp.concatenate([jnp.where(visible, s[h * HALF : (h + 1) * HALF], NEG) for h in range(HB)], 0)
        m_old = m_s[g, rows]
        mx = s[:, :128]
        for t in range(1, BK // 128):
            mx = jnp.maximum(mx, s[:, t * 128 : (t + 1) * 128])
        m_new = jnp.maximum(m_old, jnp.max(mx, axis=1, keepdims=True))
        alpha = jnp.exp(m_old - m_new)
        m_s[g, rows] = m_new
        parts, total = [], l_s[g, rows] * alpha
        for t in range(BK // 128):
            p = jnp.exp(s[:, t * 128 : (t + 1) * 128] - m_new)
            total = total + p
            parts.append(p.astype(BF))
        l_s[g, rows] = total
        v = kvs[pl.ds(start, BK), HD:]
        o = jnp.dot(jnp.concatenate(parts, 1), v, preferred_element_type=F32)
        acc[g, rows] = acc[g, rows] * jnp.concatenate([alpha, alpha], 1) + o

    def item(masked, i, carry):
        g, start = place_of(i)
        g_next, start_next = place_of(jnp.minimum(i + 1, n_items - 1))
        n = HEADS // HB
        s = ahead[...]
        for j in range(n):
            after = scores(g, start, j + 1) if j + 1 < n else scores(g_next, start_next, 0)
            fold(g, start, j, s, masked)
            s = after
        ahead[...] = s
        return carry

    ahead[...] = scores(*place_of(0), 0)
    lax.fori_loop(0, NY * per - 1, functools.partial(item, False), 0)
    for cp in second:
        cp.wait()
    lax.fori_loop(NY * per - 1, n_whole, functools.partial(item, False), 0)
    lax.fori_loop(n_whole, n_items, functools.partial(item, True), 0)

    lane = lax.broadcasted_iota(jnp.int32, (HALF, 128), 1)
    lane8 = lax.broadcasted_iota(jnp.int32, (8, 128), 1)
    pick = pl.ds(15, 4, stride=16)
    for dy in range(NY):
        lse = [jnp.zeros((HALF, 128), F32)] * 2
        few = jnp.zeros((8, 128), F32)
        for h in range(HEADS):
            rows = slice(h * HALF, (h + 1) * HALF)
            for half in range(2):
                g = half * NY + ((y + dy) & (NY - 1))
                total = jnp.maximum(jnp.sum(l_s[g, rows], axis=1, keepdims=True), 1e-30)
                value = m_s[g, rows] + jnp.log(total)
                lse[half] = jnp.where(lane == h, value, lse[half])
                o = acc[g, rows] * (1.0 / total)
                out, at = (outs[NY], 0) if dy == 2 and half else (outs[dy], half * HALF)
                out[at : at + HALF, h * HD : (h + 1) * HD] = o.astype(BF)
                stage[half * HALF : (half + 1) * HALF] = o[:, :128]
                stage[(2 + half) * HALF : (3 + half) * HALF] = o[:, 128:]
                stage[(4 + half) * HALF : (5 + half) * HALF] = value
            got = [stage[pl.ds(i * 2 * HALF + 15, 8, stride=16), :] for i in range(3)]
            few_outs[dy][:16, h * HD : (h + 1) * HD] = jnp.concatenate(
                [jnp.concatenate(got[:2], 1), jnp.zeros((8, HD), F32)], 0
            ).astype(BF)
            few = jnp.where(lane8 == h, got[2], few)
        block = jnp.concatenate(lse, 0).T[:HEADS]
        for out, blk, at in ((outs[NY], block, HALF) if dy == 2 else (outs[dy], block, 2 * HALF), (few_outs[dy], few, 16)):
            for p, v in enumerate(packed(blk)):
                out[at : at + 16, p * 128 : (p + 1) * 128] = v
            out[at : at + 16, 384:] = jnp.zeros((16, HEADS * HD - 384), BF)
        for i in (dy, NY + 1 + dy) + ((NY,) if dy == 2 else ()):
            to_hbm[i].start()
    for cp in to_hbm:
        cp.wait()


def attention(place, qs, kv):
    tok, width = qs[0].shape
    layout = [e for _, e in kv]
    hbm = pl.BlockSpec(memory_space=pl.ANY)
    spans = [(r0, r0 + rows) for e in layout for _, (_, _, _, r0, rows) in e]
    n_copies = 2 * NY + sum(len([h for h in (0, 1) if max(a, h * HALF) < min(b, (h + 1) * HALF)]) for a, b in spans)
    shapes = [jax.ShapeDtypeStruct((n, width), BF) for n in (tok + 16, tok + 16, HALF, tok + 16, HALF + 16)]
    shapes += [jax.ShapeDtypeStruct((32, width), BF)] * NY
    return pl.pallas_call(
        functools.partial(attention_kernel, layout),
        in_specs=[pl.BlockSpec(memory_space=pltpu.SMEM)] + [hbm] * (len(qs) + len(kv)),
        out_specs=[hbm] * len(shapes),
        out_shape=shapes,
        scratch_shapes=[
            pltpu.VMEM((2 * SPAN, 2 * HD), BF),
            pltpu.VMEM((2 * NY, HALF, width), BF),
            pltpu.VMEM((2 * NY, HEADS * HALF, HD), F32),
            pltpu.VMEM((2 * NY, HEADS * HALF, 128), F32),
            pltpu.VMEM((2 * NY, HEADS * HALF, 128), F32),
            pltpu.VMEM((6 * HALF, 128), F32),
            pltpu.VMEM((HB * HALF, BK), F32),
            pltpu.SemaphoreType.DMA((n_copies,)),
            pltpu.SemaphoreType.DMA((len(shapes),)),
        ]
        + [pltpu.VMEM(o.shape, BF) for o in shapes],
        compiler_params=pltpu.CompilerParams(vmem_limit_bytes=56 * 2**20),
        cost_estimate=pl.CostEstimate(flops=10**10, bytes_accessed=8 * 2**20, transcendentals=10**7),
    )(place, *qs, *[a for a, _ in kv])


def by_row(block, rows):
    if rows == 16:
        return jnp.concatenate([block, jnp.zeros((8, 128), F32)], 0)
    return jnp.concatenate([block, jnp.zeros((120, 128), F32)], 0).T


def join_kernel(rows, place, r0, r1, r2, r3, g_ref, keep_ref, send_ref):
    xl, c = place[2], place[3]
    refs = (r0, r1, r2, r3)
    blocks = []
    for r in refs:
        parts = [r[rows : rows + 16, p * 128 : (p + 1) * 128].astype(F32) for p in range(3)]
        blocks.append((parts[0] + parts[1] + parts[2])[:8])
    m = functools.reduce(jnp.maximum, blocks)
    exps = [jnp.exp(b - m) for b in blocks]
    total = exps[0] + exps[1] + exps[2] + exps[3]
    weights = [by_row(e / total, rows) for e in exps]
    low = lax.broadcasted_iota(jnp.int32, (rows, 128), 1) < 64
    for pair in range(HEADS // 2):
        quarters = []
        for h in (2 * pair, 2 * pair + 1):
            for t in range(2):
                cols = slice(h * HD + t * 128, h * HD + (t + 1) * 128)
                o = jnp.zeros((rows, 128), F32)
                for r, w in zip(refs, weights):
                    o = o + r[:rows, cols].astype(F32) * w[:, h : h + 1]
                quarters.append(jax.nn.sigmoid(g_ref[:, cols].astype(F32)) * o)
        cols = slice(pair * 128, (pair + 1) * 128)
        for t in range(2):
            a, b = quarters[t], quarters[2 + t]
            first = jnp.where(low, a, pltpu.roll(b, 64, 1))
            second = jnp.where(low, pltpu.roll(a, 64, 1), b)
            keep_ref[t ^ xl, :, cols] = jnp.where(c == 0, first, second).astype(BF)
            send_ref[t ^ xl, :, cols] = jnp.where(c == 0, second, first).astype(BF)


def join(place, parts, g):
    rows, width = g.shape
    vm = pl.BlockSpec(memory_space=pltpu.VMEM)
    half = jax.ShapeDtypeStruct((NX, rows, width // TEAM), BF)
    return pl.pallas_call(
        functools.partial(join_kernel, rows),
        in_specs=[pl.BlockSpec(memory_space=pltpu.SMEM)] + [vm] * 5,
        out_specs=[vm, vm],
        out_shape=[half, half],
        compiler_params=pltpu.CompilerParams(vmem_limit_bytes=24 * 2**20),
    )(place, *parts, g)


def project_kernel(rows, parts, place, a_ref, b_ref, *refs):
    w_refs, (keep_ref, send_ref, ws, sems) = refs[: len(parts)], refs[len(parts) :]
    z, dp = place[1], place[4]
    loads = []
    for w, (part, flip, first) in zip(w_refs, parts):
        for i in range(w.shape[0]):
            head = (z + ORDER[first + i] + NZ) & (NZ - 1)
            row = part * HEADS * HALF + head * HALF + (dp ^ flip) * 32
            for t in range(2):
                groups = slice(2 * t, 2 * t + 2)
                dst = ws.at[groups, pl.ds(pl.multiple_of(row, 32), 32)]
                loads.append(pltpu.make_async_copy(w.at[i, groups], dst, sems.at[len(loads)]))
    for load in loads[::2] + loads[1::2]:
        load.start()
    x = jnp.concatenate([jnp.concatenate([a_ref[t], b_ref[t]], 0) for t in range(NX)], 1)
    step = ws.shape[2]
    for i in range(ws.shape[0]):
        if i % 2 == 0:
            for load in loads[i // 2 :: 2]:
                load.wait()
        cols = slice(i * step, (i + 1) * step)
        out = jnp.dot(x, ws[i], preferred_element_type=F32)
        keep_ref[:, cols] = out[:rows]
        send_ref[:, cols] = out[rows:].astype(BF)


def project(place, a, b, weights):
    rows = a.shape[1]
    _, groups, _, step = weights[0][0].shape
    width = groups * step
    vm = pl.BlockSpec(memory_space=pltpu.VMEM)
    hbm = pl.BlockSpec(memory_space=pl.ANY)
    n = sum(w.shape[0] for w, _ in weights)
    return pl.pallas_call(
        functools.partial(project_kernel, rows, [p for _, p in weights]),
        in_specs=[pl.BlockSpec(memory_space=pltpu.SMEM), vm, vm] + [hbm] * len(weights),
        out_specs=[vm, vm],
        out_shape=[jax.ShapeDtypeStruct((rows, width), F32), jax.ShapeDtypeStruct((rows, width), BF)],
        scratch_shapes=[pltpu.VMEM((groups, NX * HEADS * HALF, step), BF), pltpu.SemaphoreType.DMA((2 * n,))],
        compiler_params=pltpu.CompilerParams(vmem_limit_bytes=24 * 2**20),
    )(place, a, b, *[w for w, _ in weights])


def lens_kernel(who, x_ref, w_ref, *refs):
    out_ref = refs[-1]
    got = jnp.dot(x_ref[...], w_ref[...], preferred_element_type=F32)
    for i in range(out_ref.shape[0]):
        for j in range(NX):
            at = (i * NX + j) * NZ * 8
            out_ref[i, :, j, 0] = got[at : at + NZ * 8].reshape(NZ, 8, -1)


def lens(who, x, weight, before=None):
    ys = 2
    tile = ys * NX * NZ * 8
    rows, depth = x.shape
    vocab = weight.shape[1]
    extra = [] if before is None else [before]
    return pl.pallas_call(
        lens_kernel,
        grid_spec=pltpu.PrefetchScalarGridSpec(
            num_scalar_prefetch=1,
            grid=(rows // tile,),
            in_specs=[pl.BlockSpec((tile, depth), lambda i, w: (i, 0)), pl.BlockSpec((depth, vocab), lambda i, w: (0, 0))]
            + [pl.BlockSpec(memory_space=pl.ANY)] * len(extra),
            out_specs=pl.BlockSpec((ys, NZ, NX, 1, 8, vocab), lambda i, w: (i, 0, 0, w[0], 0, 0)),
        ),
        out_shape=jax.ShapeDtypeStruct((NY, NZ, NX, NC, 8, vocab), F32),
        input_output_aliases={} if before is None else {3: 0},
        compiler_params=pltpu.CompilerParams(vmem_limit_bytes=28 * 2**20),
        cost_estimate=pl.CostEstimate(flops=2 * rows * weight.size, bytes_accessed=6 * 2**20, transcendentals=0),
    )(who, x, weight, *extra)


def short_conv(prefix, rows, taps):
    lag = taps.shape[0] - 1
    extended = jnp.concatenate([prefix, rows], 0).astype(F32)
    total = jnp.zeros(rows.shape, F32)
    for t in range(lag + 1):
        total = total + taps[t].astype(F32) * extended[lag - t : lag - t + rows.shape[0]]
    return total


def hidden_rows(resid, rims, taps, me, last):
    lag = taps.shape[0] - 1
    count = NY * NZ * NX * NC
    names = ("y", "z", "xl", "c")
    low = lax.ppermute(rims[:lag], names, [(i, i + 1) for i in range(count - 1)])
    high = lax.ppermute(rims[lag:], names, [(i + 1, i) for i in range(count - 1)])
    high = jnp.where(me == last, resid[HALF - lag : HALF], high)
    conv = jnp.concatenate([short_conv(low, resid[:HALF], taps), short_conv(high, resid[HALF:], taps)], 0)
    return (resid.astype(F32) + jax.nn.silu(conv)).astype(BF)


def shift(x, axis, by):
    count = {"y": NY, "z": NZ, "xl": NX, "c": NC}[axis]
    return lax.ppermute(x, axis, [(i, (i + by) % count) for i in range(count)])


def body(resid, conv_weight, queries, keys, values, gates, out_weight, norm_gain, lens_weight):
    y, z, xl, c = (lax.axis_index(a) for a in ("y", "z", "xl", "c"))
    me = ((y * NZ + z) * NX + xl) * NC + c
    dp = lax.axis_index("dp")
    place = jnp.stack([y, z, xl, c, dp]).astype(jnp.int32)
    tok, width = resid.shape
    few = lambda a: jnp.pad(a.reshape(8, 16, -1)[:, 15], ((0, 8), (0, 0)))

    w_half = jnp.where(dp == 0, out_weight[:32], out_weight[32:])
    w_block = jnp.concatenate([w_half[:, i * 512 : (i + 1) * 512] for i in range(width // 512)], 0)

    kv_own = lax.optimization_barrier(jnp.concatenate([keys, values], 1))
    q_up, q_down = shift(queries, "y", -1), shift(queries, "y", 1)
    q_far = [shift(q_down[:HALF], "y", 1), shift(q_up[HALF:], "y", -1)]
    load = jnp.concatenate([kv_own, shift(kv_own, "xl", 1), w_block], 0)
    n_kv, half = 2 * tok, load.shape[0] // 2
    both = lambda dz: [(0, (dz, 0, 0, 0, tok)), (tok, (dz, 1, 0, 0, tok))]
    held = [(load, n_kv, both(0))]
    fwd = bwd = load
    for s in range(1, NZ // 2):
        fwd, bwd = shift(fwd, "z", 1), shift(bwd, "z", -1)
        if s < NZ // 2 - 1:
            held += [(fwd, n_kv, both(-s)), (bwd, n_kv, both(s))]
    taps = conv_weight.astype(F32)
    blocks = resid.reshape(8, 16, width)
    conv_few = sum(taps[t] * blocks[:, 15 - t].astype(F32) for t in range(conv_weight.shape[0]))
    hidden_few = (blocks[:, 15].astype(F32) + jax.nn.silu(conv_few)).astype(BF)
    g_few = few(gates)
    fwd, bwd, q_up, q_down, hidden_few, g_few, place, *q_far = lax.optimization_barrier(
        (fwd, bwd, q_up, q_down, hidden_few, g_few, place, *q_far)
    )
    held += [(fwd, n_kv, both(1 - NZ // 2)), (bwd, n_kv, both(NZ // 2 - 1))]
    far_low, far_high = shift(fwd[:half], "z", 1), shift(bwd[half:], "z", -1)
    cut = half - tok
    held.append((far_low, half, [(0, (4, 0, 0, 0, tok)), (tok, (4, 1, 0, 0, cut))]))
    held.append((far_high, tok - cut, [(0, (4, 1, 0, cut, tok - cut))]))
    q_team = [queries, q_up, q_down] + q_far

    kv = []
    for group in (held[:SWAP], held[SWAP:]):
        entries, base = [], 0
        for piece, n, spans in group:
            kv.append((piece, spans))
            entries += [(base + at, (dz, dx, 1, r0, rows)) for at, (dz, dx, _, r0, rows) in spans]
            base += n
        kv.append((shift(jnp.concatenate([p[:n] for p, n, _ in group], 0), "c", 1), entries))

    shape = (NZ, width // 512, 32, 512)
    w_own = jnp.concatenate([p[n_kv:] for p, _, _ in held[:-2]] + [far_high[tok - cut :]], 0).reshape(shape)
    across = lambda a: lax.ppermute(a, ("xl", "dp"), [(i, 3 - i) for i in range(4)])
    w_x, w_d = shift(w_own, "xl", 1), across(w_own)
    place, _ = lax.optimization_barrier((place, w_own))
    got = attention(place, q_team, kv)
    main, lead = got[: NY + 1], got[NY + 1 :]
    to_team = lambda a: [a[0], shift(a[1], "y", 1), shift(a[2], "y", 2), shift(a[3], "y", -1)]
    spread = lambda a, axes, n: lax.all_to_all(jnp.broadcast_to(a[None], (n,) + a.shape), axes, 0, 0).reshape(-1, width)

    w_far = [across(w_x[: NZ // 2]), shift(w_d[NZ // 2 :], "xl", 1)]
    weights = [(w_own, (0, 0, 0)), (w_x, (1, 0, 0)), (w_d, (1, 1, 0))]
    weights += [(w_far[0], (0, 1, 0)), (w_far[1], (0, 1, NZ // 2))]
    lead = to_team(lead)
    f_keep, f_send = join(place, lead, g_few)
    f_own, f_other = project(place, f_keep, shift(f_send, "c", 1), weights)
    far = [shift(main[2], "y", 1), shift(main[4], "y", -1)]
    f_other = shift(f_other, "c", 1)
    lag = conv_weight.shape[0] - 1
    rims = jnp.concatenate([resid[HALF - lag : HALF], resid[2 * HALF - lag :]], 0)
    f_other, rims, *far = lax.optimization_barrier((f_other, rims, *far))
    far = [shift(far[0], "y", 1), shift(far[1], "y", -1)]
    near = [shift(main[1], "y", 1), shift(main[3], "y", -1)]
    rows = (hidden_few.astype(F32) + (f_own + f_other.astype(F32))[:8]).astype(BF).astype(F32)
    normed = (rows * lax.rsqrt(jnp.mean(rows * rows, axis=-1, keepdims=True) + 1e-6) * norm_gain).astype(BF)
    per_z = spread(normed, "z", NZ)
    per_z, *near = lax.optimization_barrier((per_z, *near))
    copies = jnp.broadcast_to(per_z[None], (NY * NX,) + per_z.shape)
    _, *far = lax.optimization_barrier((copies, *far))
    main = [main[0], near[0], jnp.concatenate(far, 0), near[1]]
    every = lax.all_to_all(copies, ("y", "xl"), 0, 0).reshape(-1, width)

    hidden = hidden_rows(resid, rims, conv_weight, me, NY * NZ * NX * NC - 1)
    keep, send = join(place, main, gates)
    p_own, p_other = project(place, keep, shift(send, "c", 1), weights)
    mixed = (hidden.astype(F32) + p_own + shift(p_other, "c", 1).astype(F32)).astype(BF)
    every, mixed = lax.optimization_barrier((every, mixed))

    theirs = shift(every, "c", 1)
    who = c.astype(jnp.int32).reshape(1)
    logits = lens(who, every, lens_weight)
    logits = lens(1 - who, theirs, lens_weight, logits)
    return mixed, logits.reshape(-1, lens_weight.shape[1])


def solution(mesh):
    fine = Mesh(mesh.devices.reshape(NY, NZ, NX, NC, -1), ("y", "z", "xl", "c", "dp"))
    rows = P(("dp", "y", "z", "xl", "c"), None)
    return jax.shard_map(
        body,
        mesh=fine,
        in_specs=(rows, P(), rows, rows, rows, rows, P(("z", "xl", "c"), None), P(), P(None, ("y", "z", "xl", "c"))),
        out_specs=(rows, P("dp", ("y", "z", "xl", "c"))),
        check_vma=False,
    )
```
